32 devices in a mesh: groups: 2 (over y), seq: 4 (over x, core), tensor: 4 (over z).
Axes of the slice: x: 2, y: 2, z: 4, core: 2. Of those that a mesh axis runs over, the one named last changes fastest.
Arguments:
- layer_input: bfloat16 [4096, 4096], P(('groups', 'seq'), 'tensor'), parts along dimension 0, may hold values from -6 to 6
- out_grad: bfloat16 [4096, 4096], P(('groups', 'seq'), 'tensor'), parts along dimension 0, may hold values from -6 to 6
- gate_pre: bfloat16 [4096, 14336], P(('groups', 'seq'), 'tensor'), parts along dimension 0, may hold values from -6 to 6
- up_pre: bfloat16 [4096, 14336], P(('groups', 'seq'), 'tensor'), parts along dimension 0, may hold values from -6 to 6
- w_down: bfloat16 [14336, 4096], P('tensor', 'seq'), may hold values from -0.046875 to 0.046875
- proj_in: bfloat16 [4096, 128], P('tensor'), may hold values from -0.09375 to 0.09375
- proj_ff: bfloat16 [14336, 192], P('tensor'), may hold values from -0.046875 to 0.046875
- proj_down: bfloat16 [4096, 64], replicated, may hold values from -0.09375 to 0.09375
- lengths: int32 [8], P('groups'), parts along dimension 0, may hold values from 1 to 1024, 2048 in all
- slots: int32 [8], P('groups'), parts along dimension 0, may hold values from 0 to 3, each once
Outputs:
- owned_sketches: float32 [8, 3, 64, 64], P('groups', None, 'tensor', 'seq'), parts along dimension 0
The draws below stay inside these ranges and needn't reach their ends.
There are 2 independent parts, one for each index of `groups`. The reference program is written for one: setup_inputs(seed, part) draws one part's arguments, and reference() takes and returns one part's arrays. A program takes and returns all parts, laid end to end along the dimension named above; an argument that names none is the same for every part. Nothing has to cross between parts.
Inputs may be any that keep to these rules, and one draw needn't show every extreme that they name: The lengths of the 4 sequences sum to 2048; the longest is exactly 1024. `slots`: A permutation of the 4 output rows.
All inputs are finite; a program needn't handle non-finite values.
Results may differ from the reference program's by a relative error of at most 0.0029.
Values may be sent and summed in bfloat16 or wider, within the bound.
No kernel may reach another device: no remote copies, remote signals or barrier semaphores. Data moves between devices by JAX's collectives and lax.ppermute only.
A program may use at most 128 MiB of HBM per device.

```python
import math
import jax
import jax.numpy as jnp
import numpy as np
from jax import lax

D = 4096
FF = 14336
TOK_DEV = 512
EXAMPLES = 4
TOKENS = 2048
MOST = 1024


def levels(key, extent, cuts, smallest, top_value):
    def one(axis_at, blocks):
        heights = jax.random.uniform(jax.random.fold_in(jax.random.fold_in(key, 6), axis_at), (blocks,), jnp.float32, smallest / len(cuts), top_value / len(cuts))
        return jnp.repeat(jnp.exp(heights), extent[axis_at] // blocks).reshape((-1,) + (1,) * (len(extent) - axis_at - 1))

    gain = one(*cuts[0])
    for cut in cuts[1:]:
        gain = gain * one(*cut)
    return gain


def length_profile(number_of, total, limit, lean):
    loads = [(1 << 20) // math.isqrt(rank ** lean) + 1 for rank in range(2, number_of + 1)]
    rest, counts = total - limit - (number_of - 1), [1] * (number_of - 1)
    while rest > 0:
        free = [i for i in range(number_of - 1) if counts[i] < limit]
        whole, left = sum([loads[i] for i in free]), rest
        for i in free:
            extra = min(limit - counts[i], max(1, left * loads[i] // whole), rest)
            counts[i] = counts[i] + extra
            rest = rest - extra
    return np.array([limit] + counts)


def uneven(rng, count, total, most, skew):
    if count == 2:
        one = jax.random.randint(rng, (), max(1, total - most), min(most, total - 1) + 1)
        return jnp.stack([one, total - one])
    sizes = jnp.asarray(length_profile(count, total, most, skew), jnp.int32)
    pairs = (count - 1) // 2
    donor, sink = sizes[1:1 + 2 * pairs:2], sizes[2:2 + 2 * pairs:2]
    room = jnp.minimum(donor - 1, most - sink)
    shifted = jax.random.randint(jax.random.fold_in(rng, 1), (pairs,), 0, 1 << 20) % (room + 1)
    sizes = sizes.at[1:1 + 2 * pairs:2].set(donor - shifted).at[2:2 + 2 * pairs:2].set(sink + shifted)
    return sizes[jax.random.permutation(jax.random.fold_in(rng, 2), count)]


def bell_draw(rng, extent, deviation, limit, cuts=(), kind=jnp.bfloat16):
    array = jax.random.normal(rng, extent, jnp.float32) * deviation
    if len(cuts) > 0:
        array = levels(rng, extent, cuts, -0.22, 0.18) * array
    return jnp.clip(array, min=-limit, max=limit).astype(kind)


def setup_inputs(seed: int = 0, part: int = 0) -> dict:
    arg_keys = jax.random.split(jax.random.key(seed), 11)
    part_keys = jax.random.split(jax.random.fold_in(arg_keys[10], part), 11)
    layer_input = bell_draw(part_keys[0], (TOKENS, D), 1.0, 6.0, ((0, 4), (1, 4)))
    out_grad = bell_draw(part_keys[1], (TOKENS, D), 1.0, 6.0, ((0, 4), (1, 4)))
    gate_pre = bell_draw(part_keys[2], (TOKENS, FF), 1.0, 6.0, ((0, 4), (1, 4)))
    up_pre = bell_draw(part_keys[3], (TOKENS, FF), 1.0, 6.0, ((0, 4), (1, 4)))
    w_down = bell_draw(arg_keys[4], (FF, D), FF ** -0.5, 0.046875, ((0, 4), (1, 4)))
    proj_in = bell_draw(arg_keys[5], (D, 128), D ** -0.5, 0.09375, ((0, 4),))
    proj_ff = bell_draw(arg_keys[6], (FF, 192), FF ** -0.5, 0.046875, ((0, 4),))
    proj_down = bell_draw(arg_keys[7], (D, 64), D ** -0.5, 0.09375)
    lengths = uneven(part_keys[8], EXAMPLES, TOKENS, MOST, 2).astype(jnp.int32)
    slots = jax.random.permutation(part_keys[9], EXAMPLES).astype(jnp.int32)
    return dict(layer_input=layer_input, out_grad=out_grad, gate_pre=gate_pre, up_pre=up_pre, w_down=w_down, proj_in=proj_in, proj_ff=proj_ff, proj_down=proj_down, lengths=lengths, slots=slots)


def silu_pair(gates):
    sigma = jax.nn.sigmoid(gates)
    return (gates * sigma, sigma * (1.0 + gates * (1.0 - sigma)))

def reference(layer_input, out_grad, gate_pre, up_pre, w_down, proj_in, proj_ff, proj_down, lengths, slots):
    blocks = TOKENS // TOK_DEV

    def project_block(pieces):
        inputs, grads, gates, uppers = pieces
        hidden_grad = jnp.dot(grads, w_down.T, preferred_element_type=jnp.float32)
        gate_value = gates.astype(jnp.float32)
        upper_value = uppers.astype(jnp.float32)
        activated, slope = silu_pair(gate_value)
        hidden = (activated * upper_value).astype(jnp.bfloat16)
        gate_grad = (hidden_grad * upper_value * slope).astype(jnp.bfloat16)
        up_grad = (hidden_grad * activated).astype(jnp.bfloat16)
        in_side = jnp.dot(inputs, proj_in, preferred_element_type=jnp.float32)
        down_left = jnp.dot(hidden, proj_ff[:, 128:192], preferred_element_type=jnp.float32)
        gate_right = jnp.dot(gate_grad, proj_ff[:, 0:64], preferred_element_type=jnp.float32)
        up_right = jnp.dot(up_grad, proj_ff[:, 64:128], preferred_element_type=jnp.float32)
        down_right = jnp.dot(grads, proj_down, preferred_element_type=jnp.float32)
        left_rows = jnp.concatenate([in_side, down_left], axis=1)
        right_rows = jnp.concatenate([gate_right, up_right, down_right], axis=1)
        return (left_rows, right_rows)
    left, right = lax.map(project_block, (layer_input.reshape(blocks, TOK_DEV, D), out_grad.reshape(blocks, TOK_DEV, D), gate_pre.reshape(blocks, TOK_DEV, FF), up_pre.reshape(blocks, TOK_DEV, FF)))
    left = left.reshape(TOKENS, 192)
    right = right.reshape(TOKENS, 192)
    positions = jnp.arange(TOKENS, dtype=jnp.int32)
    ends = jnp.cumsum(lengths).astype(jnp.int32)
    starts = (ends - lengths).astype(jnp.int32)
    member = ((positions[:, None] >= starts[None, :]) & (positions[:, None] < ends[None, :])).astype(jnp.float32)
    scale = lax.rsqrt(lengths.astype(jnp.float32))
    sketches = []
    for linear in range(3):
        left_part = left[:, 64 * linear:64 * linear + 64]
        right_part = right[:, 64 * linear:64 * linear + 64]
        weighted = (member[:, :, None] * left_part[:, None, :]).reshape(TOKENS, EXAMPLES * 64)
        sketch = lax.dot_general(weighted, right_part, (((0,), (0,)), ((), ())), precision=lax.Precision.HIGHEST, preferred_element_type=jnp.float32)
        sketches.append(sketch.reshape(EXAMPLES, 64, 64))
    stacked = jnp.stack(sketches, axis=1) * scale[:, None, None, None]
    return jnp.zeros_like(stacked).at[slots].set(stacked)
```

```python
import functools
import jax
import jax.numpy as jnp
from jax import lax
from jax.experimental import pallas as pl
from jax.experimental.pallas import tpu as pltpu
from jax.sharding import PartitionSpec as P

F32 = jnp.float32
BF16 = jnp.bfloat16
TILE = 256
CHUNKS = (256, 256, 256, 256, 256, 256, 256)
CALLS = (5, 1, 1)
DEPTH = 3


def silu_pair(gates):
    sigma = jax.nn.sigmoid(gates)
    return (gates * sigma, sigma * (1.0 + gates * (1.0 - sigma)))


def general(
    layer_input, out_grad, gate_pre, up_pre, w_down, proj_in, proj_ff, proj_down, lengths, slots
):
    tokens_here = layer_input.shape[0]
    tensor_count = lax.axis_size("tensor")
    share = 64 // tensor_count
    whole_down = lax.all_gather(w_down, "seq", axis=1, tiled=True)
    piece = lax.all_gather(out_grad, "tensor", axis=1, tiled=True)
    grad_total = lax.dot_general(
        piece, whole_down, (((1,), (1,)), ((), ())), preferred_element_type=F32
    )
    right_total = jnp.dot(piece, proj_down, preferred_element_type=F32)
    upper_value = up_pre.astype(F32)
    activated, slope = silu_pair(gate_pre.astype(F32))
    hidden = (activated * upper_value).astype(BF16)
    gate_grad = (grad_total * upper_value * slope).astype(BF16)
    up_grad = (grad_total * activated).astype(BF16)
    in_side = jnp.dot(layer_input, proj_in, preferred_element_type=F32)
    down_left = jnp.dot(hidden, proj_ff[:, 128:192], preferred_element_type=F32)
    gate_right = jnp.dot(gate_grad, proj_ff[:, 0:64], preferred_element_type=F32)
    up_right = jnp.dot(up_grad, proj_ff[:, 64:128], preferred_element_type=F32)
    left_local = jnp.concatenate([in_side, down_left], axis=1)
    right_local = jnp.concatenate([gate_right, up_right], axis=1)
    tensor_place = lax.axis_index("tensor")
    left_full, right_summed = lax.psum((left_local, right_local), "tensor")
    left_mine = lax.dynamic_slice_in_dim(
        left_full.reshape(tokens_here, 3, 64), tensor_place * share, share, 2
    )
    right_all = jnp.concatenate([right_summed, right_total], axis=1).reshape(tokens_here, 3, 64)
    examples = lengths.shape[0]
    positions = lax.axis_index("seq") * tokens_here + jnp.arange(tokens_here, dtype=jnp.int32)
    ends = jnp.cumsum(lengths)
    starts = ends - lengths
    member = (
        (positions[:, None] >= starts[None, :]) & (positions[:, None] < ends[None, :])
    ).astype(F32)
    scale = lax.rsqrt(lengths.astype(F32))
    sketches = []
    for linear in range(3):
        weighted = (member[:, :, None] * left_mine[:, None, linear, :]).reshape(
            tokens_here, examples * share
        )
        sketch = lax.dot_general(
            weighted,
            right_all[:, linear, :],
            (((0,), (0,)), ((), ())),
            precision=lax.Precision.HIGHEST,
            preferred_element_type=F32,
        )
        sketches.append(sketch.reshape(examples, share * 64))
    stacked = jnp.stack(sketches, axis=1) * scale[:, None, None]
    placing = (slots[None, :] == jnp.arange(examples, dtype=jnp.int32)[:, None]).astype(F32)
    placed = jnp.dot(
        placing,
        stacked.reshape(examples, 3 * share * 64),
        precision=lax.Precision.HIGHEST,
        preferred_element_type=F32,
    )
    return lax.psum_scatter(
        placed.reshape(examples, 3, share, 64), "seq", scatter_dimension=3, tiled=True
    )


def grads_kernel(tiles, half, first, last, *refs):
    n_pairs = 1 + max(t[0] for t in tiles)
    it = iter(refs)
    take = lambda n: [next(it) for _ in range(n)]
    (scal,) = take(1)
    own, ups, downs = next(it), take(3), take(3)
    w_own, w_sib = take(2)
    pairs = [take(2) for _ in range(n_pairs)]
    gate, up, pg, pu = take(4)
    acc_in = None if first else take(2)
    if last:
        left_t, r_down, lo, hi, scale = take(5)
        keep, send = take(2)
    else:
        acc_out = take(2)
    og, wbuf, gbuf, ubuf, pbuf, acc, og_sem, sems = take(8)
    s, z, y = scal[0], scal[1], scal[2]
    n = len(tiles)

    def og_copies():
        out = [(z >= 0, own, z)]
        for k in range(1, 4):
            out.append((z >= k, ups[k - 1], z - k))
            out.append((z + k <= 3, downs[k - 1], z + k))
        return out

    for cond, ref, q in og_copies():
        @pl.when(cond)
        def _(ref=ref, q=q):
            pltpu.make_async_copy(ref, og.at[q], og_sem).start()

    def fetch(t, slot):
        for i, (pair, row, off, mine) in enumerate(tiles):
            @pl.when(t == i)
            def _(pair=pair, row=row, off=off, mine=mine):
                h = y if mine else 1 - y
                at = pl.multiple_of(h * half + off, 128)
                rows = pl.ds(at, TILE)
                here = pl.ds(row, TILE)
                a, b = pairs[pair]
                for j, src in enumerate(
                    (w_own.at[rows], w_sib.at[rows], a.at[here], b.at[here])
                ):
                    pltpu.make_async_copy(src, wbuf.at[slot, j], sems.at[slot]).start()
                pltpu.make_async_copy(gate.at[:, rows], gbuf.at[slot], sems.at[slot]).start()
                pltpu.make_async_copy(up.at[:, rows], ubuf.at[slot], sems.at[slot]).start()
                pltpu.make_async_copy(pg.at[rows], pbuf.at[slot, 0], sems.at[slot]).start()
                pltpu.make_async_copy(pu.at[rows], pbuf.at[slot, 1], sems.at[slot]).start()

    def arrive(slot):
        rows = pl.ds(0, TILE)
        for j in range(4):
            pltpu.make_async_copy(w_own.at[rows], wbuf.at[slot, j], sems.at[slot]).wait()
        pltpu.make_async_copy(gate.at[:, rows], gbuf.at[slot], sems.at[slot]).wait()
        pltpu.make_async_copy(up.at[:, rows], ubuf.at[slot], sems.at[slot]).wait()
        pltpu.make_async_copy(pg.at[rows], pbuf.at[slot, 0], sems.at[slot]).wait()
        pltpu.make_async_copy(pu.at[rows], pbuf.at[slot, 1], sems.at[slot]).wait()

    fetch(jnp.int32(0), 0)
    if first:
        acc[...] = jnp.zeros_like(acc)
    else:
        acc[0] = acc_in[0][...]
        acc[1] = acc_in[1][...]
    for q in range(4):
        pltpu.make_async_copy(own, og.at[q], og_sem).wait()

    @pl.loop(0, n)
    def _(t):
        slot = lax.rem(t, 2)
        @pl.when(t + 1 < n)
        def _():
            fetch(t + 1, 1 - slot)
        arrive(slot)
        for m in range(2):
            toks = pl.ds(m * 256, 256)
            total = None
            for j in range(4):
                part = lax.dot_general(
                    og[s ^ j, toks, :],
                    wbuf[slot, j],
                    (((1,), (1,)), ((), ())),
                    preferred_element_type=F32,
                )
                total = part if total is None else total + part
            activated, slope = silu_pair(gbuf[slot, toks, :].astype(F32))
            gate_grad = (total * ubuf[slot, toks, :].astype(F32) * slope).astype(BF16)
            up_grad = (total * activated).astype(BF16)
            acc[0, toks, :] += jnp.dot(gate_grad, pbuf[slot, 0], preferred_element_type=F32)
            acc[1, toks, :] += jnp.dot(up_grad, pbuf[slot, 1], preferred_element_type=F32)

    if not last:
        acc_out[0][...] = acc[0]
        acc_out[1][...] = acc[1]
        return
    tokens = acc.shape[1]
    where = s * tokens + lax.broadcasted_iota(jnp.int32, (tokens, 256), 0)
    weight = jnp.where((where >= lo[...]) & (where < hi[...]), scale[...], 0.0)
    for l in range(3):
        right = (r_down[...] if l == 2 else acc[l]) * weight
        m = jnp.dot(
            left_t[pl.ds(64 * l, 64), :],
            right,
            precision=lax.Precision.HIGHEST,
            preferred_element_type=F32,
        )
        even = lax.rem(s, 2) == 0
        keep[l] = jnp.where(even, m[:, :128], m[:, 128:])
        send[l] = jnp.where(even, m[:, 128:], m[:, :128])


def grads_call(tiles, half, scal, og_parts, weights, pairs, streams, acc, tail):
    tokens, depth = og_parts[0].shape
    first, last = acc is None, tail is not None
    any_spec = pl.BlockSpec(memory_space=pl.ANY)
    vmem = pl.BlockSpec(memory_space=pltpu.VMEM)
    args = [scal, *og_parts, *weights, *[a for p in pairs for a in p], *streams]
    specs = [pl.BlockSpec(memory_space=pltpu.SMEM)] + [any_spec] * (len(args) - 1)
    if not first:
        args += list(acc)
        specs += [vmem] * 2
    if last:
        args += list(tail)
        specs += [vmem] * len(tail)
        outs = [jax.ShapeDtypeStruct((3, 64, 128), F32)] * 2
    else:
        outs = [jax.ShapeDtypeStruct((tokens, 256), F32)] * 2
    flops = 2 * len(tiles) * TILE * tokens * (4 * depth + 512)
    return pl.pallas_call(
        functools.partial(grads_kernel, tiles, half, first, last),
        out_shape=outs,
        in_specs=specs,
        out_specs=[vmem] * 2,
        scratch_shapes=[
            pltpu.VMEM((4, tokens, depth), BF16),
            pltpu.VMEM((2, 4, TILE, depth), BF16),
            pltpu.VMEM((2, tokens, TILE), BF16),
            pltpu.VMEM((2, tokens, TILE), BF16),
            pltpu.VMEM((2, 2, TILE, 256), BF16),
            pltpu.VMEM((2, tokens, 256), F32),
            pltpu.SemaphoreType.DMA,
            pltpu.SemaphoreType.DMA((2,)),
        ],
        compiler_params=pltpu.CompilerParams(vmem_limit_bytes=40 * 1024 * 1024),
        cost_estimate=pl.CostEstimate(
            flops=flops,
            bytes_accessed=2 * (4 * tokens * depth + len(tiles) * TILE * (4 * depth + 2 * tokens)),
            transcendentals=len(tiles) * TILE * tokens,
        ),
    )(*args)


def local(
    layer_input, out_grad, gate_pre, up_pre, w_down, proj_in, proj_ff, proj_down, lengths, slots
):
    tokens = layer_input.shape[0]
    depth = out_grad.shape[1]
    units = w_down.shape[0]
    half = units // 2
    y, s, z = (lax.axis_index(a) for a in ("groups", "seq", "tensor"))
    scal = jnp.stack([s, z, y]).astype(jnp.int32)

    over_x = lambda a: lax.ppermute(a, "seq", [(i, i ^ 2) for i in range(4)])
    over_c = lambda a: lax.ppermute(a, "seq", [(i, i ^ 1) for i in range(4)])
    over_y = lambda a: lax.ppermute(a, "groups", [(0, 1), (1, 0)])
    over_z = lambda a, k: lax.ppermute(a, "tensor", [(i, i ^ k) for i in range(4)])

    count = len(CHUNKS)
    offs = [sum(CHUNKS[:k]) for k in range(count)]
    srcs = [
        lax.dynamic_slice_in_dim(w_down, y * half + offs[k], CHUNKS[k], 0) for k in range(count)
    ]
    r, rc, ry, yc = ([None] * count for _ in range(4))
    for k in range(DEPTH):
        r[k] = over_x(srcs[k])
    w_sib = over_c(w_down)

    ups, downs = [], []
    rise = fall = out_grad
    z_at = {1: 1, 3: 2, 5: 3}

    def z_step(k, rise, fall):
        rise = lax.ppermute(rise, "tensor", [(i, i + 1) for i in range(k - 1, 3)])
        fall = lax.ppermute(fall, "tensor", [(i + 1, i) for i in range(0, 4 - k)])
        return rise, fall

    rise, fall = z_step(1, rise, fall)

    upper = up_pre.astype(F32)
    activated, _ = silu_pair(gate_pre.astype(F32))
    hidden = (activated * upper).astype(BF16)
    in_side = jnp.dot(layer_input, proj_in, preferred_element_type=F32)
    down_left = jnp.dot(hidden, proj_ff[:, 128:192], preferred_element_type=F32)
    left_t = lax.psum(jnp.concatenate([in_side, down_left], axis=1).T, "tensor")

    column = jnp.arange(64, dtype=jnp.int32)[:, None]
    lane = jnp.arange(256, dtype=jnp.int32)[None, :]
    source = (2 * ((lane // 64) % 2) + lane // 128) * 16 + lane % 16
    spread = (column == source).astype(BF16)
    expand = lambda a: jnp.dot(a, spread, preferred_element_type=F32).astype(BF16)
    pg, pu = expand(proj_ff[:, 0:64]), expand(proj_ff[:, 64:128])
    down_rows = lax.dynamic_slice_in_dim(proj_down, z * depth, depth, 0)
    r_down = jnp.dot(out_grad, expand(down_rows), preferred_element_type=F32)
    ends = jnp.cumsum(lengths)
    pick = slots[:, None] == (lane // 16) % 4
    by_lane = lambda a: jnp.sum(jnp.where(pick, a[:, None], jnp.zeros((), a.dtype)), 0, keepdims=True)
    lo, hi = by_lane(ends - lengths), by_lane(ends)
    scale = by_lane(lax.rsqrt(lengths.astype(F32)))

    for k in range(count):
        items = {"r": r[k]}
        if k >= 2:
            items["y"] = ry[k - 2]
        if k + DEPTH < count:
            items["w"] = srcs[k + DEPTH]
        if k in z_at:
            items["z"] = (rise, fall)
        items = lax.optimization_barrier(items)
        r[k] = items["r"]
        ry[k] = over_y(r[k])
        rc[k] = over_c(r[k])
        if k >= 2:
            ry[k - 2] = items["y"]
            yc[k - 2] = over_c(ry[k - 2])
        if k + DEPTH < count:
            r[k + DEPTH] = over_x(items["w"])
        if k in z_at:
            rise, fall = items["z"]
            ups.append(rise)
            downs.append(fall)
            if z_at[k] < 3:
                rise, fall = z_step(z_at[k] + 1, rise, fall)
    for k in (count - 2, count - 1):
        yc[k] = over_c(ry[k])

    acc = None
    begin = 0
    for c, n in enumerate(CALLS):
        pairs, tiles = [], []
        for k in range(begin, begin + n):
            for mine in (True, False):
                for row in range(0, CHUNKS[k], TILE):
                    tiles.append((len(pairs), row, offs[k] + row, mine))
                pairs.append((r[k], rc[k]) if mine else (ry[k], yc[k]))
        begin += n
        last = c == len(CALLS) - 1
        acc = grads_call(
            tuple(tiles), half, scal, (out_grad, *ups, *downs), (w_down, w_sib), pairs,
            (gate_pre, up_pre, pg, pu), acc,
            (left_t, r_down, lo, hi, scale) if last else None,
        )
    keep, send = acc
    x = s // 2
    total = (keep + over_c(send)).reshape(3, 64, 2, 64)
    part = lambda a, axis, at: lax.dynamic_index_in_dim(a, at, axis, keepdims=False)
    total = part(total, 2, x) + over_x(part(total, 2, 1 - x))
    total = total.reshape(3, 2, 32, 64)
    total = part(total, 1, z // 2) + over_z(part(total, 1, 1 - z // 2), 2)
    total = total.reshape(3, 2, 16, 64)
    total = part(total, 1, z % 2) + over_z(part(total, 1, 1 - z % 2), 1)
    return total.reshape(3, 16, 4, 16).transpose(2, 0, 1, 3)


def solution(mesh):
    placed = (
        P(("groups", "seq"), "tensor"),
        P(("groups", "seq"), "tensor"),
        P(("groups", "seq"), "tensor"),
        P(("groups", "seq"), "tensor"),
        P("tensor", "seq"),
        P("tensor", None),
        P("tensor", None),
        P(),
        P("groups"),
        P("groups"),
    )
    small = (mesh.shape["groups"], mesh.shape["seq"], mesh.shape["tensor"]) == (2, 4, 4)
    return jax.shard_map(
        local if small else general,
        mesh=mesh,
        in_specs=placed,
        out_specs=P("groups", None, "tensor", "seq"),
        check_vma=False,
    )
```

```python
import functools
import jax
import jax.numpy as jnp
from jax import lax
from jax.experimental import pallas as pl
from jax.experimental.pallas import tpu as pltpu
from jax.sharding import PartitionSpec as P

F32 = jnp.float32
BF16 = jnp.bfloat16
TILE = 256
CHUNKS = (256, 256, 256, 256, 256, 256, 256)


def silu_pair(gates):
    sigma = jax.nn.sigmoid(gates)
    return (gates * sigma, sigma * (1.0 + gates * (1.0 - sigma)))


def general(
    layer_input, out_grad, gate_pre, up_pre, w_down, proj_in, proj_ff, proj_down, lengths, slots
):
    tokens_here = layer_input.shape[0]
    tensor_count = lax.axis_size("tensor")
    share = 64 // tensor_count
    whole_down = lax.all_gather(w_down, "seq", axis=1, tiled=True)
    piece = lax.all_gather(out_grad, "tensor", axis=1, tiled=True)
    grad_total = lax.dot_general(
        piece, whole_down, (((1,), (1,)), ((), ())), preferred_element_type=F32
    )
    right_total = jnp.dot(piece, proj_down, preferred_element_type=F32)
    upper_value = up_pre.astype(F32)
    activated, slope = silu_pair(gate_pre.astype(F32))
    hidden = (activated * upper_value).astype(BF16)
    gate_grad = (grad_total * upper_value * slope).astype(BF16)
    up_grad = (grad_total * activated).astype(BF16)
    in_side = jnp.dot(layer_input, proj_in, preferred_element_type=F32)
    down_left = jnp.dot(hidden, proj_ff[:, 128:192], preferred_element_type=F32)
    gate_right = jnp.dot(gate_grad, proj_ff[:, 0:64], preferred_element_type=F32)
    up_right = jnp.dot(up_grad, proj_ff[:, 64:128], preferred_element_type=F32)
    left_local = jnp.concatenate([in_side, down_left], axis=1)
    right_local = jnp.concatenate([gate_right, up_right], axis=1)
    tensor_place = lax.axis_index("tensor")
    left_full, right_summed = lax.psum((left_local, right_local), "tensor")
    left_mine = lax.dynamic_slice_in_dim(
        left_full.reshape(tokens_here, 3, 64), tensor_place * share, share, 2
    )
    right_all = jnp.concatenate([right_summed, right_total], axis=1).reshape(tokens_here, 3, 64)
    examples = lengths.shape[0]
    positions = lax.axis_index("seq") * tokens_here + jnp.arange(tokens_here, dtype=jnp.int32)
    ends = jnp.cumsum(lengths)
    starts = ends - lengths
    member = (
        (positions[:, None] >= starts[None, :]) & (positions[:, None] < ends[None, :])
    ).astype(F32)
    scale = lax.rsqrt(lengths.astype(F32))
    sketches = []
    for linear in range(3):
        weighted = (member[:, :, None] * left_mine[:, None, linear, :]).reshape(
            tokens_here, examples * share
        )
        sketch = lax.dot_general(
            weighted,
            right_all[:, linear, :],
            (((0,), (0,)), ((), ())),
            precision=lax.Precision.HIGHEST,
            preferred_element_type=F32,
        )
        sketches.append(sketch.reshape(examples, share * 64))
    stacked = jnp.stack(sketches, axis=1) * scale[:, None, None]
    placing = (slots[None, :] == jnp.arange(examples, dtype=jnp.int32)[:, None]).astype(F32)
    placed = jnp.dot(
        placing,
        stacked.reshape(examples, 3 * share * 64),
        precision=lax.Precision.HIGHEST,
        preferred_element_type=F32,
    )
    return lax.psum_scatter(
        placed.reshape(examples, 3, share, 64), "seq", scatter_dimension=3, tiled=True
    )


def move_kernel(moves, n_in, *refs):
    scal, ins, refs = refs[0], refs[1 : 1 + n_in], refs[1 + n_in :]
    outs, (buf, sem) = refs[:-2], refs[-2:]
    y, at, steps = scal[2], 0, []
    for i, (src, lead, row, dst, to, rows) in enumerate(moves):
        a = ins[src].at[y, pl.ds(row, rows)] if lead else ins[src].at[pl.ds(row, rows)]
        mid = buf.at[pl.ds(at, rows)]
        steps.append(
            (
                pltpu.make_async_copy(a, mid, sem.at[0, i]),
                pltpu.make_async_copy(mid, outs[dst].at[pl.ds(to, rows)], sem.at[1, i]),
            )
        )
        at += rows
    for a, _ in steps:
        a.start()
    for a, b in steps:
        a.wait()
        b.start()
    for _, b in steps:
        b.wait()


def move(scal, ins, moves, out_rows):
    width, kind = ins[0].shape[-1], ins[0].dtype
    hbm = pl.BlockSpec(memory_space=pltpu.HBM)
    total = sum(m[-1] for m in moves)
    return pl.pallas_call(
        functools.partial(move_kernel, tuple(moves), len(ins)),
        out_shape=[jax.ShapeDtypeStruct((rows, width), kind) for rows in out_rows],
        in_specs=[pl.BlockSpec(memory_space=pltpu.SMEM)] + [hbm] * len(ins),
        out_specs=[hbm] * len(out_rows),
        scratch_shapes=[
            pltpu.VMEM((total, width), kind),
            pltpu.SemaphoreType.DMA((2, len(moves))),
        ],
        compiler_params=pltpu.CompilerParams(vmem_limit_bytes=60 * 1024 * 1024),
        cost_estimate=pl.CostEstimate(
            flops=0, bytes_accessed=4 * total * width, transcendentals=0
        ),
    )(scal, *ins)


def join(scal, pieces):
    moves, at = [], 0
    for i, piece in enumerate(pieces):
        moves.append((i, False, 0, 0, at, piece.shape[0]))
        at += piece.shape[0]
    return move(scal, pieces, moves, [at])[0]


def grads_kernel(tiles, half, first, last, *refs):
    n_pairs = 1 + max(t[0] for t in tiles)
    it = iter(refs)
    take = lambda n: [next(it) for _ in range(n)]
    (scal,) = take(1)
    (gathered,) = take(1)
    w_own, w_sib = take(2)
    pairs = [take(2) for _ in range(n_pairs)]
    gate, up, pg, pu = take(4)
    acc_in = None if first else take(2)
    if last:
        left_t, r_down, lo, hi, scale = take(5)
        keep, send = take(2)
    else:
        acc_out = take(2)
    og, wbuf, gbuf, ubuf, pbuf, grads, og_sem, sems, p_sem = take(9)
    s, y = scal[0], scal[2]
    n = len(tiles)

    def fetch(t, slot, with_grad=False):
        for i, (pair, row, off, mine) in enumerate(tiles):
            if with_grad and i:
                break

            @pl.when(t == i)
            def _(pair=pair, row=row, off=off, mine=mine, i=i):
                h = y if mine else 1 - y
                at = pl.multiple_of(h * half + off, 128)
                rows = pl.ds(at, TILE)
                here = pl.ds(row, TILE)
                a, b = pairs[pair]
                for j, src in enumerate(
                    (w_own.at[rows], w_sib.at[rows], a.at[here], b.at[here])
                ):
                    if with_grad:
                        pltpu.make_async_copy(gathered.at[s ^ j], og.at[s ^ j], og_sem.at[j]).start()
                    pltpu.make_async_copy(src, wbuf.at[slot, j], sems.at[slot, j]).start()
                pltpu.make_async_copy(gate.at[:, rows], gbuf.at[slot], sems.at[slot, 4]).start()
                pltpu.make_async_copy(up.at[:, rows], ubuf.at[slot], sems.at[slot, 5]).start()
                mine_p = pl.ds(i * TILE, TILE)
                pltpu.make_async_copy(pg.at[rows], pbuf.at[0, mine_p], p_sem).start()
                pltpu.make_async_copy(pu.at[rows], pbuf.at[1, mine_p], p_sem).start()

    def weights_arrive(slot, j):
        pltpu.make_async_copy(w_own.at[pl.ds(0, TILE)], wbuf.at[slot, j], sems.at[slot, j]).wait()

    def dots(slot, before):
        total = None
        for j in range(4):
            before(j)
            part = lax.dot_general(
                og[s ^ j],
                wbuf[slot, j],
                (((1,), (1,)), ((), ())),
                preferred_element_type=F32,
            )
            total = part if total is None else total + part
        return total

    def finish(t, slot, total):
        activated, slope = silu_pair(gbuf[slot].astype(F32))
        columns = pl.ds(pl.multiple_of(t * TILE, 128), TILE)
        grads[0, :, columns] = (total * ubuf[slot].astype(F32) * slope).astype(BF16)
        grads[1, :, columns] = (total * activated).astype(BF16)

    def streams_arrive(slot):
        rows = pl.ds(0, TILE)
        pltpu.make_async_copy(gate.at[:, rows], gbuf.at[slot], sems.at[slot, 4]).wait()
        pltpu.make_async_copy(up.at[:, rows], ubuf.at[slot], sems.at[slot, 5]).wait()

    def first_quarter(j):
        weights_arrive(0, j)
        pltpu.make_async_copy(gathered.at[j], og.at[j], og_sem.at[j]).wait()

    fetch(jnp.int32(0), 0, True)
    if n > 1:
        fetch(jnp.int32(1), 1)
    total = dots(0, first_quarter)
    streams_arrive(0)
    finish(0, 0, total)

    @pl.loop(1, n)
    def _(t):
        slot = lax.rem(t, 2)
        @pl.when(t + 1 < n)
        def _():
            fetch(t + 1, 1 - slot)
        for j in range(4):
            weights_arrive(slot, j)
        streams_arrive(slot)
        finish(t, slot, dots(slot, lambda j: None))

    every = pl.ds(0, n * TILE)
    pltpu.make_async_copy(pg.at[every], pbuf.at[0], p_sem).wait()
    pltpu.make_async_copy(pu.at[every], pbuf.at[1], p_sem).wait()
    acc = [jnp.dot(grads[i], pbuf[i], preferred_element_type=F32) for i in range(2)]
    if not first:
        acc = [a + b[...] for a, b in zip(acc, acc_in)]
    if not last:
        acc_out[0][...] = acc[0]
        acc_out[1][...] = acc[1]
        return
    tokens = acc[0].shape[0]
    where = s * tokens + lax.broadcasted_iota(jnp.int32, (tokens, 256), 0)
    weight = jnp.where((where >= lo[...]) & (where < hi[...]), scale[...], 0.0)
    for l in range(3):
        right = (r_down[...] if l == 2 else acc[l]) * weight
        m = jnp.dot(
            left_t[pl.ds(64 * l, 64), :],
            right,
            precision=lax.Precision.HIGHEST,
            preferred_element_type=F32,
        )
        even = lax.rem(s, 2) == 0
        keep[l] = jnp.where(even, m[:, :128], m[:, 128:])
        send[l] = jnp.where(even, m[:, 128:], m[:, :128])


def grads_call(tiles, half, scal, gathered, weights, pairs, streams, acc, tail):
    _, tokens, depth = gathered.shape
    first, last = acc is None, tail is not None
    hbm = pl.BlockSpec(memory_space=pltpu.HBM)
    vmem = pl.BlockSpec(memory_space=pltpu.VMEM)
    args = [scal, gathered, *weights, *[a for p in pairs for a in p], *streams]
    specs = [pl.BlockSpec(memory_space=pltpu.SMEM)] + [hbm] * (len(args) - 1)
    if not first:
        args += list(acc)
        specs += [vmem] * 2
    if last:
        args += list(tail)
        specs += [vmem] * len(tail)
        outs = [jax.ShapeDtypeStruct((3, 64, 128), F32)] * 2
    else:
        outs = [jax.ShapeDtypeStruct((tokens, 256), F32)] * 2
    units = len(tiles) * TILE
    return pl.pallas_call(
        functools.partial(grads_kernel, tiles, half, first, last),
        out_shape=outs,
        in_specs=specs,
        out_specs=[vmem] * 2,
        scratch_shapes=[
            pltpu.VMEM((4, tokens, depth), BF16),
            pltpu.VMEM((2, 4, TILE, depth), BF16),
            pltpu.VMEM((2, tokens, TILE), BF16),
            pltpu.VMEM((2, tokens, TILE), BF16),
            pltpu.VMEM((2, units, 256), BF16),
            pltpu.VMEM((2, tokens, units), BF16),
            pltpu.SemaphoreType.DMA((4,)),
            pltpu.SemaphoreType.DMA((2, 6)),
            pltpu.SemaphoreType.DMA,
        ],
        compiler_params=pltpu.CompilerParams(vmem_limit_bytes=60 * 1024 * 1024),
        cost_estimate=pl.CostEstimate(
            flops=2 * units * tokens * (4 * depth + 512),
            bytes_accessed=2 * (4 * tokens * depth + units * (4 * depth + 2 * tokens)),
            transcendentals=units * tokens,
        ),
    )(*args)


def local(
    layer_input, out_grad, gate_pre, up_pre, w_down, proj_in, proj_ff, proj_down, lengths, slots
):
    tokens = layer_input.shape[0]
    depth = out_grad.shape[1]
    units = w_down.shape[0]
    half = units // 2
    y, s, z = (lax.axis_index(a) for a in ("groups", "seq", "tensor"))
    scal = jnp.stack([s, z, y]).astype(jnp.int32)

    over_x = lambda a: lax.ppermute(a, "seq", [(i, i ^ 2) for i in range(4)])
    over_c = lambda a: lax.ppermute(a, "seq", [(i, i ^ 1) for i in range(4)])
    over_y = lambda a: lax.ppermute(a, "groups", [(0, 1), (1, 0)])
    over_z = lambda a, k: lax.ppermute(a, "tensor", [(i, i ^ k) for i in range(4)])

    count = len(CHUNKS)
    offs = [sum(CHUNKS[:k]) for k in range(count)]
    r, ry = [None] * count, [None] * count
    tie = lax.optimization_barrier
    halves = w_down.reshape(2, half, depth)
    cut = lambda ks: move(
        scal,
        [halves],
        [(0, True, offs[k], i, 0, CHUNKS[k]) for i, k in enumerate(ks)],
        [CHUNKS[k] for k in ks],
    )

    gathered = lax.all_gather(out_grad, "tensor", axis=0, tiled=False)
    r[0] = over_x(cut([0])[0])
    srcs = [None] + list(cut(range(1, count)))
    now = srcs[2:]
    r[1] = over_x(srcs[1])
    w_sib = over_c(w_down)

    column = jnp.arange(64, dtype=jnp.int32)[:, None]
    lane = jnp.arange(256, dtype=jnp.int32)[None, :]
    source = (2 * ((lane // 64) % 2) + lane // 128) * 16 + lane % 16
    spread = (column == source).astype(BF16)
    expand = lambda a: jnp.dot(a, spread, preferred_element_type=F32).astype(BF16)
    ends = jnp.cumsum(lengths)
    pick = slots[:, None] == (lane // 16) % 4
    by_lane = lambda a: jnp.sum(jnp.where(pick, a[:, None], jnp.zeros((), a.dtype)), 0, keepdims=True)
    lo, hi = by_lane(ends - lengths), by_lane(ends)
    scale = by_lane(lax.rsqrt(lengths.astype(F32)))

    swap_after = {
        3: ((0, 0), (0, 1), (1, 0), (1, 1), (2, 0)),
        6: ((2, 1), (3, 0), (3, 1), (4, 0), (4, 1), (5, 0), (5, 1), (6, 0)),
    }
    pairs, where = [], {}

    def swap(members):
        rows = 0
        for k, far in members:
            for row in range(0, CHUNKS[k], TILE):
                where[(k, far, row)] = (len(pairs), rows)
                rows += TILE
        got = [ry[k] if far else r[k] for k, far in members]
        got = got[0] if len(got) == 1 else join(scal, got)
        pairs.append((got, over_c(got)))

    for k in range(count):
        final = k == count - 1
        gate = {"now": now, "r": r[k]}
        if k == 0:
            gate["left"] = (layer_input, gate_pre, up_pre)
        if k == 2:
            gate["left"] = left_t
        if k == count - 2:
            gate["side"] = (proj_ff, proj_down, left_t)
        if final:
            gate["side"], gate["left"] = side, left_t
        if k == 1:
            gate["sib"] = w_sib
        if k >= 2:
            gate["y"] = ry[k - 2]
        if final:
            gate["y5"], gate["all"] = ry[k - 1], gathered
        gate = tie(gate)
        now, r[k] = gate["now"], gate["r"]
        if k + 2 < count:
            r[k + 2] = over_x(now[0])
            now = now[1:]
        if k >= 2:
            ry[k - 2] = gate["y"]
        if k == 1:
            w_sib = gate["sib"]
        ry[k] = over_y(r[k])
        if k == 0:
            tokens_in, gates, uppers = gate["left"]
            activated, _ = silu_pair(gates.astype(F32))
            hidden = (activated * uppers.astype(F32)).astype(BF16)
            in_side = jnp.dot(tokens_in, proj_in, preferred_element_type=F32)
            down_left = jnp.dot(hidden, proj_ff[:, 128:192], preferred_element_type=F32)
            left_t = jnp.concatenate([in_side, down_left], axis=1).T
        if k == 2:
            left_t = gate["left"]
        if k == count - 2:
            ff, down, left_t = gate["side"]
            left_t = (left_t, over_z(left_t.astype(BF16), 1))
            down_rows = lax.dynamic_slice_in_dim(down, z * depth, depth, 0)
            side = (
                expand(ff[:, 0:64]),
                expand(ff[:, 64:128]),
                jnp.dot(out_grad, expand(down_rows), preferred_element_type=F32),
            )
        if final:
            pg, pu, r_down = gate["side"]
            left_t = gate["left"][0] + gate["left"][1].astype(F32)
            left_t = left_t + over_z(left_t.astype(BF16), 2).astype(F32)
            ry[k - 1], gathered = gate["y5"], gate["all"]
        if k in swap_after:
            swap(swap_after[k])

    def grads(members, acc, tail=None):
        used, tiles = [], []
        for k, far in members:
            for row in range(0, CHUNKS[k], TILE):
                pair, at = where[(k, far, row)]
                if pair not in used:
                    used.append(pair)
                tiles.append((used.index(pair), at, offs[k] + row, not far))
        return grads_call(
            tuple(tiles), half, scal, gathered, (w_down, w_sib), [pairs[p] for p in used],
            (gate_pre, up_pre, pg, pu), acc, tail,
        )

    gathered, left_t = tie((gathered, left_t))
    acc = grads(swap_after[3], None)
    ry[6], acc = tie((ry[6], acc))
    swap(((6, 1),))
    acc = grads(swap_after[6] + ((6, 1),), acc, (left_t, r_down, lo, hi, scale))
    keep, send = acc
    x = s // 2
    total = (keep + over_c(send)).reshape(3, 64, 2, 64)
    part = lambda a, axis, at: lax.dynamic_index_in_dim(a, at, axis, keepdims=False)
    total = part(total, 2, x) + over_x(part(total, 2, 1 - x))
    total = total.reshape(3, 2, 32, 64)
    total = part(total, 1, z // 2) + over_z(part(total, 1, 1 - z // 2), 2)
    total = total.reshape(3, 2, 16, 64)
    total = part(total, 1, z % 2) + over_z(part(total, 1, 1 - z % 2), 1)
    return total.reshape(3, 16, 4, 16).transpose(2, 0, 1, 3)


def solution(mesh):
    placed = (
        P(("groups", "seq"), "tensor"),
        P(("groups", "seq"), "tensor"),
        P(("groups", "seq"), "tensor"),
        P(("groups", "seq"), "tensor"),
        P("tensor", "seq"),
        P("tensor", None),
        P("tensor", None),
        P(),
        P("groups"),
        P("groups"),
    )
    small = (mesh.shape["groups"], mesh.shape["seq"], mesh.shape["tensor"]) == (2, 4, 4)
    return jax.shard_map(
        local if small else general,
        mesh=mesh,
        in_specs=placed,
        out_specs=P("groups", None, "tensor", "seq"),
        check_vma=False,
    )
```

```python
import functools
import jax
import jax.numpy as jnp
from jax import lax
from jax.experimental import pallas as pl
from jax.experimental.pallas import tpu as pltpu
from jax.sharding import PartitionSpec as P

F32 = jnp.float32
BF16 = jnp.bfloat16
TILE = 256
CHUNKS = (256, 256, 256, 256, 256, 256, 256)


def silu_pair(gates):
    sigma = jax.nn.sigmoid(gates)
    return (gates * sigma, sigma * (1.0 + gates * (1.0 - sigma)))


def general(
    layer_input, out_grad, gate_pre, up_pre, w_down, proj_in, proj_ff, proj_down, lengths, slots
):
    tokens_here = layer_input.shape[0]
    tensor_count = lax.axis_size("tensor")
    share = 64 // tensor_count
    whole_down = lax.all_gather(w_down, "seq", axis=1, tiled=True)
    piece = lax.all_gather(out_grad, "tensor", axis=1, tiled=True)
    grad_total = lax.dot_general(
        piece, whole_down, (((1,), (1,)), ((), ())), preferred_element_type=F32
    )
    right_total = jnp.dot(piece, proj_down, preferred_element_type=F32)
    upper_value = up_pre.astype(F32)
    activated, slope = silu_pair(gate_pre.astype(F32))
    hidden = (activated * upper_value).astype(BF16)
    gate_grad = (grad_total * upper_value * slope).astype(BF16)
    up_grad = (grad_total * activated).astype(BF16)
    in_side = jnp.dot(layer_input, proj_in, preferred_element_type=F32)
    down_left = jnp.dot(hidden, proj_ff[:, 128:192], preferred_element_type=F32)
    gate_right = jnp.dot(gate_grad, proj_ff[:, 0:64], preferred_element_type=F32)
    up_right = jnp.dot(up_grad, proj_ff[:, 64:128], preferred_element_type=F32)
    left_local = jnp.concatenate([in_side, down_left], axis=1)
    right_local = jnp.concatenate([gate_right, up_right], axis=1)
    tensor_place = lax.axis_index("tensor")
    left_full, right_summed = lax.psum((left_local, right_local), "tensor")
    left_mine = lax.dynamic_slice_in_dim(
        left_full.reshape(tokens_here, 3, 64), tensor_place * share, share, 2
    )
    right_all = jnp.concatenate([right_summed, right_total], axis=1).reshape(tokens_here, 3, 64)
    examples = lengths.shape[0]
    positions = lax.axis_index("seq") * tokens_here + jnp.arange(tokens_here, dtype=jnp.int32)
    ends = jnp.cumsum(lengths)
    starts = ends - lengths
    member = (
        (positions[:, None] >= starts[None, :]) & (positions[:, None] < ends[None, :])
    ).astype(F32)
    scale = lax.rsqrt(lengths.astype(F32))
    sketches = []
    for linear in range(3):
        weighted = (member[:, :, None] * left_mine[:, None, linear, :]).reshape(
            tokens_here, examples * share
        )
        sketch = lax.dot_general(
            weighted,
            right_all[:, linear, :],
            (((0,), (0,)), ((), ())),
            precision=lax.Precision.HIGHEST,
            preferred_element_type=F32,
        )
        sketches.append(sketch.reshape(examples, share * 64))
    stacked = jnp.stack(sketches, axis=1) * scale[:, None, None]
    placing = (slots[None, :] == jnp.arange(examples, dtype=jnp.int32)[:, None]).astype(F32)
    placed = jnp.dot(
        placing,
        stacked.reshape(examples, 3 * share * 64),
        precision=lax.Precision.HIGHEST,
        preferred_element_type=F32,
    )
    return lax.psum_scatter(
        placed.reshape(examples, 3, share, 64), "seq", scatter_dimension=3, tiled=True
    )


def move_kernel(moves, n_in, *refs):
    scal, ins, refs = refs[0], refs[1 : 1 + n_in], refs[1 + n_in :]
    outs, (buf, sem) = refs[:-2], refs[-2:]
    y, at, steps = scal[2], 0, []
    for i, (src, lead, row, dst, to, rows) in enumerate(moves):
        a = ins[src].at[y, pl.ds(row, rows)] if lead else ins[src].at[pl.ds(row, rows)]
        mid = buf.at[pl.ds(at, rows)]
        steps.append(
            (
                pltpu.make_async_copy(a, mid, sem.at[0, i]),
                pltpu.make_async_copy(mid, outs[dst].at[pl.ds(to, rows)], sem.at[1, i]),
            )
        )
        at += rows
    for a, _ in steps:
        a.start()
    for a, b in steps:
        a.wait()
        b.start()
    for _, b in steps:
        b.wait()


def move(scal, ins, moves, out_rows):
    width, kind = ins[0].shape[-1], ins[0].dtype
    hbm = pl.BlockSpec(memory_space=pltpu.HBM)
    total = sum(m[-1] for m in moves)
    return pl.pallas_call(
        functools.partial(move_kernel, tuple(moves), len(ins)),
        out_shape=[jax.ShapeDtypeStruct((rows, width), kind) for rows in out_rows],
        in_specs=[pl.BlockSpec(memory_space=pltpu.SMEM)] + [hbm] * len(ins),
        out_specs=[hbm] * len(out_rows),
        scratch_shapes=[
            pltpu.VMEM((total, width), kind),
            pltpu.SemaphoreType.DMA((2, len(moves))),
        ],
        compiler_params=pltpu.CompilerParams(vmem_limit_bytes=60 * 1024 * 1024),
        cost_estimate=pl.CostEstimate(
            flops=0, bytes_accessed=4 * total * width, transcendentals=0
        ),
    )(scal, *ins)


def join(scal, pieces):
    moves, at = [], 0
    for i, piece in enumerate(pieces):
        moves.append((i, False, 0, 0, at, piece.shape[0]))
        at += piece.shape[0]
    return move(scal, pieces, moves, [at])[0]


def grads_kernel(tiles, half, first, last, *refs):
    n_pairs = 1 + max(t[0] for t in tiles)
    it = iter(refs)
    take = lambda n: [next(it) for _ in range(n)]
    (scal,) = take(1)
    (gathered,) = take(1)
    w_own, w_sib = take(2)
    pairs = [take(2) for _ in range(n_pairs)]
    gate, up, pg, pu = take(4)
    acc_in = None if first else take(2)
    if last:
        left_t, r_down, lo, hi, scale = take(5)
        keep, send = take(2)
    else:
        acc_out = take(2)
    og, wbuf, gbuf, ubuf, pbuf, grads, og_sem, sems, p_sem = take(9)
    s, y = scal[0], scal[2]
    n = len(tiles)

    def fetch(t, slot, with_grad=False):
        for i, (pair, row, off, mine) in enumerate(tiles):
            if with_grad and i:
                break

            @pl.when(t == i)
            def _(pair=pair, row=row, off=off, mine=mine, i=i):
                h = y if mine else 1 - y
                at = pl.multiple_of(h * half + off, 128)
                rows = pl.ds(at, TILE)
                here = pl.ds(row, TILE)
                a, b = pairs[pair]
                for j, src in enumerate(
                    (w_own.at[rows], w_sib.at[rows], a.at[here], b.at[here])
                ):
                    if with_grad:
                        pltpu.make_async_copy(gathered.at[s ^ j], og.at[s ^ j], og_sem.at[j]).start()
                    pltpu.make_async_copy(src, wbuf.at[slot, j], sems.at[slot, j]).start()
                pltpu.make_async_copy(gate.at[:, rows], gbuf.at[slot], sems.at[slot, 4]).start()
                pltpu.make_async_copy(up.at[:, rows], ubuf.at[slot], sems.at[slot, 5]).start()
                mine_p = pl.ds(i * TILE, TILE)
                pltpu.make_async_copy(pg.at[rows], pbuf.at[0, mine_p], p_sem).start()
                pltpu.make_async_copy(pu.at[rows], pbuf.at[1, mine_p], p_sem).start()

    def weights_arrive(slot, j):
        pltpu.make_async_copy(w_own.at[pl.ds(0, TILE)], wbuf.at[slot, j], sems.at[slot, j]).wait()

    def dots(slot, before):
        total = None
        for j in range(4):
            before(j)
            part = lax.dot_general(
                og[s ^ j],
                wbuf[slot, j],
                (((1,), (1,)), ((), ())),
                preferred_element_type=F32,
            )
            total = part if total is None else total + part
        return total

    def finish(t, slot, total):
        activated, slope = silu_pair(gbuf[slot].astype(F32))
        columns = pl.ds(pl.multiple_of(t * TILE, 128), TILE)
        grads[0, :, columns] = (total * ubuf[slot].astype(F32) * slope).astype(BF16)
        grads[1, :, columns] = (total * activated).astype(BF16)

    def streams_arrive(slot):
        rows = pl.ds(0, TILE)
        pltpu.make_async_copy(gate.at[:, rows], gbuf.at[slot], sems.at[slot, 4]).wait()
        pltpu.make_async_copy(up.at[:, rows], ubuf.at[slot], sems.at[slot, 5]).wait()

    def first_quarter(j):
        weights_arrive(0, j)
        pltpu.make_async_copy(gathered.at[j], og.at[j], og_sem.at[j]).wait()
        if j == 2 and n > 1:
            fetch(jnp.int32(1), 1)

    fetch(jnp.int32(0), 0, True)
    total = dots(0, first_quarter)
    streams_arrive(0)
    finish(0, 0, total)

    @pl.loop(1, n)
    def _(t):
        slot = lax.rem(t, 2)
        @pl.when(t + 1 < n)
        def _():
            fetch(t + 1, 1 - slot)
        for j in range(4):
            weights_arrive(slot, j)
        streams_arrive(slot)
        finish(t, slot, dots(slot, lambda j: None))

    every = pl.ds(0, n * TILE)
    pltpu.make_async_copy(pg.at[every], pbuf.at[0], p_sem).wait()
    pltpu.make_async_copy(pu.at[every], pbuf.at[1], p_sem).wait()
    acc = [jnp.dot(grads[i], pbuf[i], preferred_element_type=F32) for i in range(2)]
    if not first:
        acc = [a + b[...] for a, b in zip(acc, acc_in)]
    if not last:
        acc_out[0][...] = acc[0]
        acc_out[1][...] = acc[1]
        return
    tokens = acc[0].shape[0]
    where = s * tokens + lax.broadcasted_iota(jnp.int32, (tokens, 256), 0)
    weight = jnp.where((where >= lo[...]) & (where < hi[...]), scale[...], 0.0)
    for l in range(3):
        right = (r_down[...] if l == 2 else acc[l]) * weight
        m = jnp.dot(
            left_t[pl.ds(64 * l, 64), :],
            right,
            precision=lax.Precision.HIGHEST,
            preferred_element_type=F32,
        )
        even = lax.rem(s, 2) == 0
        keep[l] = jnp.where(even, m[:, :128], m[:, 128:])
        send[l] = jnp.where(even, m[:, 128:], m[:, :128])


def grads_call(tiles, half, scal, gathered, weights, pairs, streams, acc, tail):
    _, tokens, depth = gathered.shape
    first, last = acc is None, tail is not None
    hbm = pl.BlockSpec(memory_space=pltpu.HBM)
    vmem = pl.BlockSpec(memory_space=pltpu.VMEM)
    args = [scal, gathered, *weights, *[a for p in pairs for a in p], *streams]
    specs = [pl.BlockSpec(memory_space=pltpu.SMEM)] + [hbm] * (len(args) - 1)
    if not first:
        args += list(acc)
        specs += [vmem] * 2
    if last:
        args += list(tail)
        specs += [vmem] * len(tail)
        outs = [jax.ShapeDtypeStruct((3, 64, 128), F32)] * 2
    else:
        outs = [jax.ShapeDtypeStruct((tokens, 256), F32)] * 2
    units = len(tiles) * TILE
    return pl.pallas_call(
        functools.partial(grads_kernel, tiles, half, first, last),
        out_shape=outs,
        in_specs=specs,
        out_specs=[vmem] * 2,
        scratch_shapes=[
            pltpu.VMEM((4, tokens, depth), BF16),
            pltpu.VMEM((2, 4, TILE, depth), BF16),
            pltpu.VMEM((2, tokens, TILE), BF16),
            pltpu.VMEM((2, tokens, TILE), BF16),
            pltpu.VMEM((2, units, 256), BF16),
            pltpu.VMEM((2, tokens, units), BF16),
            pltpu.SemaphoreType.DMA((4,)),
            pltpu.SemaphoreType.DMA((2, 6)),
            pltpu.SemaphoreType.DMA,
        ],
        compiler_params=pltpu.CompilerParams(vmem_limit_bytes=60 * 1024 * 1024),
        cost_estimate=pl.CostEstimate(
            flops=2 * units * tokens * (4 * depth + 512),
            bytes_accessed=2 * (4 * tokens * depth + units * (4 * depth + 2 * tokens)),
            transcendentals=units * tokens,
        ),
    )(*args)


def local(
    layer_input, out_grad, gate_pre, up_pre, w_down, proj_in, proj_ff, proj_down, lengths, slots
):
    tokens = layer_input.shape[0]
    depth = out_grad.shape[1]
    units = w_down.shape[0]
    half = units // 2
    y, s, z = (lax.axis_index(a) for a in ("groups", "seq", "tensor"))
    scal = jnp.stack([s, z, y]).astype(jnp.int32)

    over_x = lambda a: lax.ppermute(a, "seq", [(i, i ^ 2) for i in range(4)])
    over_c = lambda a: lax.ppermute(a, "seq", [(i, i ^ 1) for i in range(4)])
    over_y = lambda a: lax.ppermute(a, "groups", [(0, 1), (1, 0)])
    over_z = lambda a, k: lax.ppermute(a, "tensor", [(i, i ^ k) for i in range(4)])

    count = len(CHUNKS)
    offs = [sum(CHUNKS[:k]) for k in range(count)]
    r, ry = [None] * count, [None] * count
    tie = lax.optimization_barrier
    halves = w_down.reshape(2, half, depth)
    cut = lambda ks: move(
        scal,
        [halves],
        [(0, True, offs[k], i, 0, CHUNKS[k]) for i, k in enumerate(ks)],
        [CHUNKS[k] for k in ks],
    )

    gathered = lax.all_gather(out_grad, "tensor", axis=0, tiled=False)
    r[0] = over_x(cut([0])[0])
    srcs = [None] + list(cut(range(1, count)))
    now = srcs[2:]
    r[1] = over_x(srcs[1])
    w_sib = over_c(w_down)

    column = jnp.arange(64, dtype=jnp.int32)[:, None]
    lane = jnp.arange(256, dtype=jnp.int32)[None, :]
    source = (2 * ((lane // 64) % 2) + lane // 128) * 16 + lane % 16
    spread = (column == source).astype(BF16)
    expand = lambda a: jnp.dot(a, spread, preferred_element_type=F32).astype(BF16)
    ends = jnp.cumsum(lengths)
    pick = slots[:, None] == (lane // 16) % 4
    by_lane = lambda a: jnp.sum(jnp.where(pick, a[:, None], jnp.zeros((), a.dtype)), 0, keepdims=True)
    lo, hi = by_lane(ends - lengths), by_lane(ends)
    scale = by_lane(lax.rsqrt(lengths.astype(F32)))

    swap_after = {
        1: (((0, 0),),),
        3: (((0, 1),),),
        6: (
            (
                (1, 0), (1, 1), (2, 0), (2, 1), (3, 0), (3, 1), (4, 0), (4, 1), (5, 0), (5, 1), (6, 0),
            ),
        ),
    }
    swapped_by = {3: 0, 5: 1}
    pairs, where = [], {}

    def swap(members):
        rows = 0
        for k, far in members:
            for row in range(0, CHUNKS[k], TILE):
                where[(k, far, row)] = (len(pairs), rows)
                rows += TILE
        got = [ry[k] if far else r[k] for k, far in members]
        got = got[0] if len(got) == 1 else join(scal, got)
        pairs.append((got, over_c(got)))

    for k in range(count):
        final = k == count - 1
        gate = {"now": now, "r": r[k]}
        if k == 0:
            gate["left"] = (layer_input, gate_pre, up_pre)
        if k == 2:
            gate["left"], gate["lanes"] = left_t, (lo, hi, scale)
        if k == count - 2:
            gate["side"] = (proj_ff, proj_down, left_t)
        if k in swapped_by:
            gate["c"] = pairs[swapped_by[k]]
        if final:
            gate["side"], gate["left"] = side, left_t
        if k == 1:
            gate["sib"] = w_sib
        if k >= 2:
            gate["y"] = ry[k - 2]
        if final:
            gate["y5"], gate["all"] = ry[k - 1], gathered
            gate["hold"] = r[1:k], ry[1 : k - 2]
        gate = tie(gate)
        now, r[k] = gate["now"], gate["r"]
        if k + 2 < count:
            r[k + 2] = over_x(now[0])
            now = now[1:]
        if k >= 2:
            ry[k - 2] = gate["y"]
        if k == 1:
            w_sib = gate["sib"]
        ry[k] = over_y(r[k])
        if k == 0:
            tokens_in, gates, uppers = gate["left"]
            activated, _ = silu_pair(gates.astype(F32))
            hidden = (activated * uppers.astype(F32)).astype(BF16)
            in_side = jnp.dot(tokens_in, proj_in, preferred_element_type=F32)
            down_left = jnp.dot(hidden, proj_ff[:, 128:192], preferred_element_type=F32)
            left_t = jnp.concatenate([in_side, down_left], axis=1).T
        if k == 2:
            left_t, (lo, hi, scale) = gate["left"], gate["lanes"]
        if k == count - 2:
            ff, down, left_t = gate["side"]
            left_t = (left_t, over_z(left_t.astype(BF16), 1))
            down_rows = lax.dynamic_slice_in_dim(down, z * depth, depth, 0)
            side = (
                expand(ff[:, 0:64]),
                expand(ff[:, 64:128]),
                jnp.dot(out_grad, expand(down_rows), preferred_element_type=F32),
            )
        if final:
            pg, pu, r_down = gate["side"]
            left_t = gate["left"][0] + gate["left"][1].astype(F32)
            left_t = left_t + over_z(left_t.astype(BF16), 2).astype(F32)
            ry[k - 1], gathered = gate["y5"], gate["all"]
            r[1:k], ry[1 : k - 2] = gate["hold"]
        if k in swapped_by:
            pairs[swapped_by[k]] = gate["c"]
        for members in swap_after.get(k, ()):
            swap(members)

    def grads(members, acc, tail=None):
        used, tiles = [], []
        for k, far in members:
            for row in range(0, CHUNKS[k], TILE):
                pair, at = where[(k, far, row)]
                if pair not in used:
                    used.append(pair)
                tiles.append((used.index(pair), at, offs[k] + row, not far))
        return grads_call(
            tuple(tiles), half, scal, gathered, (w_down, w_sib), [pairs[p] for p in used],
            (gate_pre, up_pre, pg, pu), acc, tail,
        )

    early, late = ((0, 0), (0, 1)), swap_after[6][0]
    acc = grads(early, None)
    ry[6], left_t, acc = tie((ry[6], left_t, acc))
    swap(((6, 1),))
    acc = grads(late + ((6, 1),), acc, (left_t, r_down, lo, hi, scale))
    keep, send = acc
    x = s // 2
    total = (keep + over_c(send)).reshape(3, 64, 2, 64)
    part = lambda a, axis, at: lax.dynamic_index_in_dim(a, at, axis, keepdims=False)
    total = part(total, 2, x) + over_x(part(total, 2, 1 - x))
    total = total.reshape(3, 2, 32, 64)
    total = part(total, 1, z // 2) + over_z(part(total, 1, 1 - z // 2), 2)
    total = total.reshape(3, 2, 16, 64)
    total = part(total, 1, z % 2) + over_z(part(total, 1, 1 - z % 2), 1)
    return total.reshape(3, 16, 4, 16).transpose(2, 0, 1, 3)


def solution(mesh):
    placed = (
        P(("groups", "seq"), "tensor"),
        P(("groups", "seq"), "tensor"),
        P(("groups", "seq"), "tensor"),
        P(("groups", "seq"), "tensor"),
        P("tensor", "seq"),
        P("tensor", None),
        P("tensor", None),
        P(),
        P("groups"),
        P("groups"),
    )
    small = (mesh.shape["groups"], mesh.shape["seq"], mesh.shape["tensor"]) == (2, 4, 4)
    return jax.shard_map(
        local if small else general,
        mesh=mesh,
        in_specs=placed,
        out_specs=P("groups", None, "tensor", "seq"),
        check_vma=False,
    )
```

```python
import functools
import jax
import jax.numpy as jnp
from jax import lax
from jax.experimental import pallas as pl
from jax.experimental.pallas import tpu as pltpu
from jax.sharding import PartitionSpec as P

F32 = jnp.float32
BF16 = jnp.bfloat16
TILE = 256
CHUNKS = (256, 256, 256, 256, 256, 256, 256)


def silu_pair(gates):
    sigma = jax.nn.sigmoid(gates)
    return (gates * sigma, sigma * (1.0 + gates * (1.0 - sigma)))


def general(
    layer_input, out_grad, gate_pre, up_pre, w_down, proj_in, proj_ff, proj_down, lengths, slots
):
    tokens_here = layer_input.shape[0]
    tensor_count = lax.axis_size("tensor")
    share = 64 // tensor_count
    whole_down = lax.all_gather(w_down, "seq", axis=1, tiled=True)
    piece = lax.all_gather(out_grad, "tensor", axis=1, tiled=True)
    grad_total = lax.dot_general(
        piece, whole_down, (((1,), (1,)), ((), ())), preferred_element_type=F32
    )
    right_total = jnp.dot(piece, proj_down, preferred_element_type=F32)
    upper_value = up_pre.astype(F32)
    activated, slope = silu_pair(gate_pre.astype(F32))
    hidden = (activated * upper_value).astype(BF16)
    gate_grad = (grad_total * upper_value * slope).astype(BF16)
    up_grad = (grad_total * activated).astype(BF16)
    in_side = jnp.dot(layer_input, proj_in, preferred_element_type=F32)
    down_left = jnp.dot(hidden, proj_ff[:, 128:192], preferred_element_type=F32)
    gate_right = jnp.dot(gate_grad, proj_ff[:, 0:64], preferred_element_type=F32)
    up_right = jnp.dot(up_grad, proj_ff[:, 64:128], preferred_element_type=F32)
    left_local = jnp.concatenate([in_side, down_left], axis=1)
    right_local = jnp.concatenate([gate_right, up_right], axis=1)
    tensor_place = lax.axis_index("tensor")
    left_full, right_summed = lax.psum((left_local, right_local), "tensor")
    left_mine = lax.dynamic_slice_in_dim(
        left_full.reshape(tokens_here, 3, 64), tensor_place * share, share, 2
    )
    right_all = jnp.concatenate([right_summed, right_total], axis=1).reshape(tokens_here, 3, 64)
    examples = lengths.shape[0]
    positions = lax.axis_index("seq") * tokens_here + jnp.arange(tokens_here, dtype=jnp.int32)
    ends = jnp.cumsum(lengths)
    starts = ends - lengths
    member = (
        (positions[:, None] >= starts[None, :]) & (positions[:, None] < ends[None, :])
    ).astype(F32)
    scale = lax.rsqrt(lengths.astype(F32))
    sketches = []
    for linear in range(3):
        weighted = (member[:, :, None] * left_mine[:, None, linear, :]).reshape(
            tokens_here, examples * share
        )
        sketch = lax.dot_general(
            weighted,
            right_all[:, linear, :],
            (((0,), (0,)), ((), ())),
            precision=lax.Precision.HIGHEST,
            preferred_element_type=F32,
        )
        sketches.append(sketch.reshape(examples, share * 64))
    stacked = jnp.stack(sketches, axis=1) * scale[:, None, None]
    placing = (slots[None, :] == jnp.arange(examples, dtype=jnp.int32)[:, None]).astype(F32)
    placed = jnp.dot(
        placing,
        stacked.reshape(examples, 3 * share * 64),
        precision=lax.Precision.HIGHEST,
        preferred_element_type=F32,
    )
    return lax.psum_scatter(
        placed.reshape(examples, 3, share, 64), "seq", scatter_dimension=3, tiled=True
    )


def move_kernel(moves, n_in, *refs):
    scal, ins, refs = refs[0], refs[1 : 1 + n_in], refs[1 + n_in :]
    outs, (buf, sem) = refs[:-2], refs[-2:]
    y, at, steps = scal[2], 0, []
    for i, (src, lead, row, dst, to, rows) in enumerate(moves):
        a = ins[src] if lead is None else ins[src].at[y if lead == "y" else lead]
        a = a.at[pl.ds(row, rows)]
        mid = buf.at[pl.ds(at, rows)]
        steps.append(
            (
                pltpu.make_async_copy(a, mid, sem.at[0, i]),
                pltpu.make_async_copy(mid, outs[dst].at[pl.ds(to, rows)], sem.at[1, i]),
            )
        )
        at += rows
    for a, _ in steps:
        a.start()
    for a, b in steps:
        a.wait()
        b.start()
    for _, b in steps:
        b.wait()


def move(scal, ins, moves, out_rows):
    width, kind = ins[0].shape[-1], ins[0].dtype
    hbm = pl.BlockSpec(memory_space=pltpu.HBM)
    total = sum(m[-1] for m in moves)
    return pl.pallas_call(
        functools.partial(move_kernel, tuple(moves), len(ins)),
        out_shape=[jax.ShapeDtypeStruct((rows, width), kind) for rows in out_rows],
        in_specs=[pl.BlockSpec(memory_space=pltpu.SMEM)] + [hbm] * len(ins),
        out_specs=[hbm] * len(out_rows),
        scratch_shapes=[
            pltpu.VMEM((total, width), kind),
            pltpu.SemaphoreType.DMA((2, len(moves))),
        ],
        compiler_params=pltpu.CompilerParams(vmem_limit_bytes=60 * 1024 * 1024),
        cost_estimate=pl.CostEstimate(
            flops=0, bytes_accessed=4 * total * width, transcendentals=0
        ),
    )(scal, *ins)


def join(scal, pieces):
    moves, at = [], 0
    for i, piece in enumerate(pieces):
        moves.append((i, None, 0, 0, at, piece.shape[0]))
        at += piece.shape[0]
    return move(scal, pieces, moves, [at])[0]


def grads_kernel(tiles, half, first, last, *refs):
    n_pairs = 1 + max(t[0] for t in tiles)
    it = iter(refs)
    take = lambda n: [next(it) for _ in range(n)]
    (scal,) = take(1)
    (gathered,) = take(1)
    w_own, w_sib = take(2)
    pairs = [take(2) for _ in range(n_pairs)]
    gate, up, pg, pu = take(4)
    acc_in = None if first else take(2)
    if last:
        left_t, r_down, lo, hi, scale = take(5)
        keep, send = take(2)
    else:
        acc_out = take(2)
    og, wbuf, gbuf, ubuf, pbuf, grads, og_sem, sems, p_sem = take(9)
    s, y = scal[0], scal[2]
    n = len(tiles)

    def fetch(t, slot, with_grad=False):
        for i, (pair, row, off, mine) in enumerate(tiles):
            if with_grad and i:
                break

            @pl.when(t == i)
            def _(pair=pair, row=row, off=off, mine=mine, i=i):
                h = (y, 1 - y, 0, 1)[mine]
                at = pl.multiple_of(h * half + off, 128)
                rows = pl.ds(at, TILE)
                here = pl.ds(row, TILE)
                a, b = pairs[pair]
                for j, src in enumerate(
                    (w_own.at[rows], w_sib.at[rows], a.at[here], b.at[here])
                ):
                    if with_grad:
                        pltpu.make_async_copy(gathered.at[s ^ j], og.at[s ^ j], og_sem.at[j]).start()
                    pltpu.make_async_copy(src, wbuf.at[slot, j], sems.at[slot, j]).start()
                pltpu.make_async_copy(gate.at[:, rows], gbuf.at[slot], sems.at[slot, 4]).start()
                pltpu.make_async_copy(up.at[:, rows], ubuf.at[slot], sems.at[slot, 5]).start()
                mine_p = pl.ds(i * TILE, TILE)
                pltpu.make_async_copy(pg.at[rows], pbuf.at[0, mine_p], p_sem).start()
                pltpu.make_async_copy(pu.at[rows], pbuf.at[1, mine_p], p_sem).start()

    def weights_arrive(slot, j):
        pltpu.make_async_copy(w_own.at[pl.ds(0, TILE)], wbuf.at[slot, j], sems.at[slot, j]).wait()

    def dots(slot, before):
        total = None
        for j in range(4):
            before(j)
            part = lax.dot_general(
                og[s ^ j],
                wbuf[slot, j],
                (((1,), (1,)), ((), ())),
                preferred_element_type=F32,
            )
            total = part if total is None else total + part
        return total

    def finish(t, slot, total):
        activated, slope = silu_pair(gbuf[slot].astype(F32))
        columns = pl.ds(pl.multiple_of(t * TILE, 128), TILE)
        grads[0, :, columns] = (total * ubuf[slot].astype(F32) * slope).astype(BF16)
        grads[1, :, columns] = (total * activated).astype(BF16)

    def streams_arrive(slot):
        rows = pl.ds(0, TILE)
        pltpu.make_async_copy(gate.at[:, rows], gbuf.at[slot], sems.at[slot, 4]).wait()
        pltpu.make_async_copy(up.at[:, rows], ubuf.at[slot], sems.at[slot, 5]).wait()

    def first_quarter(j):
        weights_arrive(0, j)
        pltpu.make_async_copy(gathered.at[j], og.at[j], og_sem.at[j]).wait()
        if j == 2 and n > 1:
            fetch(jnp.int32(1), 1)

    fetch(jnp.int32(0), 0, True)
    total = dots(0, first_quarter)
    streams_arrive(0)
    finish(0, 0, total)

    @pl.loop(1, n)
    def _(t):
        slot = lax.rem(t, 2)
        @pl.when(t + 1 < n)
        def _():
            fetch(t + 1, 1 - slot)
        for j in range(4):
            weights_arrive(slot, j)
        streams_arrive(slot)
        finish(t, slot, dots(slot, lambda j: None))

    every = pl.ds(0, n * TILE)
    pltpu.make_async_copy(pg.at[every], pbuf.at[0], p_sem).wait()
    pltpu.make_async_copy(pu.at[every], pbuf.at[1], p_sem).wait()
    acc = [jnp.dot(grads[i], pbuf[i], preferred_element_type=F32) for i in range(2)]
    if not first:
        acc = [a + b[...] for a, b in zip(acc, acc_in)]
    if not last:
        acc_out[0][...] = acc[0]
        acc_out[1][...] = acc[1]
        return
    tokens = acc[0].shape[0]
    where = s * tokens + lax.broadcasted_iota(jnp.int32, (tokens, 256), 0)
    weight = jnp.where((where >= lo[...]) & (where < hi[...]), scale[...], 0.0)
    for l in range(3):
        right = (r_down[...] if l == 2 else acc[l]) * weight
        m = jnp.dot(
            left_t[pl.ds(64 * l, 64), :],
            right,
            precision=lax.Precision.HIGHEST,
            preferred_element_type=F32,
        )
        even = lax.rem(s, 2) == 0
        keep[l] = jnp.where(even, m[:, :128], m[:, 128:])
        send[l] = jnp.where(even, m[:, 128:], m[:, :128])


def grads_call(tiles, half, scal, gathered, weights, pairs, streams, acc, tail):
    _, tokens, depth = gathered.shape
    first, last = acc is None, tail is not None
    hbm = pl.BlockSpec(memory_space=pltpu.HBM)
    vmem = pl.BlockSpec(memory_space=pltpu.VMEM)
    args = [scal, gathered, *weights, *[a for p in pairs for a in p], *streams]
    specs = [pl.BlockSpec(memory_space=pltpu.SMEM)] + [hbm] * (len(args) - 1)
    if not first:
        args += list(acc)
        specs += [vmem] * 2
    if last:
        args += list(tail)
        specs += [vmem] * len(tail)
        outs = [jax.ShapeDtypeStruct((3, 64, 128), F32)] * 2
    else:
        outs = [jax.ShapeDtypeStruct((tokens, 256), F32)] * 2
    units = len(tiles) * TILE
    return pl.pallas_call(
        functools.partial(grads_kernel, tiles, half, first, last),
        out_shape=outs,
        in_specs=specs,
        out_specs=[vmem] * 2,
        scratch_shapes=[
            pltpu.VMEM((4, tokens, depth), BF16),
            pltpu.VMEM((2, 4, TILE, depth), BF16),
            pltpu.VMEM((2, tokens, TILE), BF16),
            pltpu.VMEM((2, tokens, TILE), BF16),
            pltpu.VMEM((2, units, 256), BF16),
            pltpu.VMEM((2, tokens, units), BF16),
            pltpu.SemaphoreType.DMA((4,)),
            pltpu.SemaphoreType.DMA((2, 6)),
            pltpu.SemaphoreType.DMA,
        ],
        compiler_params=pltpu.CompilerParams(vmem_limit_bytes=60 * 1024 * 1024),
        cost_estimate=pl.CostEstimate(
            flops=2 * units * tokens * (4 * depth + 512),
            bytes_accessed=2 * (4 * tokens * depth + units * (4 * depth + 2 * tokens)),
            transcendentals=units * tokens,
        ),
    )(*args)


def local(
    layer_input, out_grad, gate_pre, up_pre, w_down, proj_in, proj_ff, proj_down, lengths, slots
):
    tokens = layer_input.shape[0]
    depth = out_grad.shape[1]
    units = w_down.shape[0]
    half = units // 2
    y, s, z = (lax.axis_index(a) for a in ("groups", "seq", "tensor"))
    scal = jnp.stack([s, z, y]).astype(jnp.int32)

    over_x = lambda a: lax.ppermute(a, "seq", [(i, i ^ 2) for i in range(4)])
    over_c = lambda a: lax.ppermute(a, "seq", [(i, i ^ 1) for i in range(4)])
    over_y = lambda a: lax.ppermute(a, "groups", [(0, 1), (1, 0)])
    over_z = lambda a, k: lax.ppermute(a, "tensor", [(i, i ^ k) for i in range(4)])

    count = len(CHUNKS)
    offs = [sum(CHUNKS[:k]) for k in range(count)]
    r, ry = [None] * (count + 1), [None] * count
    tie = lax.optimization_barrier
    halves = w_down.reshape(2, half, depth)
    whole = count - 1
    sources = [("y", k) for k in range(whole)] + [(0, whole), (1, whole)]
    cut = lambda picks: move(
        scal,
        [halves],
        [(0, h, offs[k], i, 0, CHUNKS[k]) for i, (h, k) in enumerate(picks)],
        [CHUNKS[k] for _, k in picks],
    )

    gathered = lax.all_gather(out_grad, "tensor", axis=0, tiled=False)
    r[0] = over_x(cut(sources[:1])[0])
    srcs = [None] + list(cut(sources[1:]))
    now = srcs[2:]
    r[1] = over_x(srcs[1])
    w_sib = over_c(w_down)

    column = jnp.arange(64, dtype=jnp.int32)[:, None]
    lane = jnp.arange(256, dtype=jnp.int32)[None, :]
    source = (2 * ((lane // 64) % 2) + lane // 128) * 16 + lane % 16
    spread = (column == source).astype(BF16)
    expand = lambda a: jnp.dot(a, spread, preferred_element_type=F32).astype(BF16)
    ends = jnp.cumsum(lengths)
    pick = slots[:, None] == (lane // 16) % 4
    by_lane = lambda a: jnp.sum(jnp.where(pick, a[:, None], jnp.zeros((), a.dtype)), 0, keepdims=True)
    lo, hi = by_lane(ends - lengths), by_lane(ends)
    scale = by_lane(lax.rsqrt(lengths.astype(F32)))

    swap_after = {
        0: ((0, 0),),
        2: ((0, 1),),
        4: ((1, 0),),
        5: ((1, 1), (2, 0), (2, 1), (3, 0), (3, 1), (4, 0)),
        6: ((4, 1), (5, 0), (5, 1), (6, 0)),
    }
    swapped_by = {2: 0, 4: 1, 6: 2}
    pairs, where = [], {}

    def swap(members, across=True):
        rows = 0
        for k, far in members:
            for row in range(0, CHUNKS[min(k, whole)], TILE):
                where[(k, far, row)] = (len(pairs), rows)
                rows += TILE
        got = [ry[k] if far else r[k] for k, far in members]
        got = got[0] if len(got) == 1 else join(scal, got)
        pairs.append((got, over_c(got)) if across else got)

    for k in range(count):
        final = k == count - 1
        gate = {"now": now, "r": r[k]}
        if k == 0:
            gate["left"] = (layer_input, gate_pre, up_pre)
        if k == 2:
            gate["left"], gate["lanes"] = left_t, (lo, hi, scale)
        if k == count - 2:
            gate["side"] = (proj_ff, proj_down, left_t)
        if k in swapped_by:
            gate["c"] = pairs[swapped_by[k]]
        if final:
            gate["side"], gate["left"] = side, left_t
        if k == 1:
            gate["sib"] = w_sib
        if k >= 2:
            gate["y"] = ry[k - 2]
        if final:
            gate["y5"], gate["all"] = ry[k - 1], gathered
            gate["join"] = pairs[3]
        gate = tie(gate)
        now, r[k] = gate["now"], gate["r"]
        if k + 2 <= count:
            r[k + 2] = over_x(now[0])
            now = now[1:]
        if k >= 2:
            ry[k - 2] = gate["y"]
        if k == 1:
            w_sib = gate["sib"]
        if not final:
            ry[k] = over_y(r[k])
        if k == 0:
            tokens_in, gates, uppers = gate["left"]
            activated, _ = silu_pair(gates.astype(F32))
            hidden = (activated * uppers.astype(F32)).astype(BF16)
            in_side = jnp.dot(tokens_in, proj_in, preferred_element_type=F32)
            down_left = jnp.dot(hidden, proj_ff[:, 128:192], preferred_element_type=F32)
            left_t = jnp.concatenate([in_side, down_left], axis=1).T
        if k == 2:
            left_t, (lo, hi, scale) = gate["left"], gate["lanes"]
        if k == count - 2:
            ff, down, left_t = gate["side"]
            left_t = (left_t, over_z(left_t.astype(BF16), 1))
            down_rows = lax.dynamic_slice_in_dim(down, z * depth, depth, 0)
            side = (
                expand(ff[:, 0:64]),
                expand(ff[:, 64:128]),
                jnp.dot(out_grad, expand(down_rows), preferred_element_type=F32),
            )
        if final:
            pg, pu, r_down = gate["side"]
            left_t = gate["left"][0] + gate["left"][1].astype(F32)
            left_t = left_t + over_z(left_t.astype(BF16), 2).astype(F32)
            ry[k - 1], gathered = gate["y5"], gate["all"]
        if k in swapped_by:
            pairs[swapped_by[k]] = gate["c"]
        if final:
            pairs[3] = (gate["join"], over_c(gate["join"]))
        if k in swap_after:
            swap(swap_after[k], k != 5)

    def grads(members, acc, tail=None):
        used, tiles = [], []
        for k, far in members:
            at_half = min(k, whole)
            for row in range(0, CHUNKS[at_half], TILE):
                pair, at = where[(k, far, row)]
                if pair not in used:
                    used.append(pair)
                half_of = far if k < whole else 2 + k - whole
                tiles.append((used.index(pair), at, offs[at_half] + row, half_of))
        return grads_call(
            tuple(tiles), half, scal, gathered, (w_down, w_sib), [pairs[p] for p in used],
            (gate_pre, up_pre, pg, pu), acc, tail,
        )

    early, late = ((0, 0), (0, 1), (1, 0)), swap_after[5] + swap_after[6]
    acc = grads(early, None)
    r[7], left_t, acc = tie((r[7], left_t, acc))
    swap(((7, 0),))
    acc = grads(late + ((7, 0),), acc, (left_t, r_down, lo, hi, scale))
    keep, send = acc
    x = s // 2
    total = (keep + over_c(send)).reshape(3, 64, 2, 64)
    part = lambda a, axis, at: lax.dynamic_index_in_dim(a, at, axis, keepdims=False)
    total = part(total, 2, x) + over_x(part(total, 2, 1 - x))
    total = total.reshape(3, 2, 32, 64)
    total = part(total, 1, z // 2) + over_z(part(total, 1, 1 - z // 2), 2)
    total = total.reshape(3, 2, 16, 64)
    total = part(total, 1, z % 2) + over_z(part(total, 1, 1 - z % 2), 1)
    return total.reshape(3, 16, 4, 16).transpose(2, 0, 1, 3)


def solution(mesh):
    placed = (
        P(("groups", "seq"), "tensor"),
        P(("groups", "seq"), "tensor"),
        P(("groups", "seq"), "tensor"),
        P(("groups", "seq"), "tensor"),
        P("tensor", "seq"),
        P("tensor", None),
        P("tensor", None),
        P(),
        P("groups"),
        P("groups"),
    )
    small = (mesh.shape["groups"], mesh.shape["seq"], mesh.shape["tensor"]) == (2, 4, 4)
    return jax.shard_map(
        local if small else general,
        mesh=mesh,
        in_specs=placed,
        out_specs=P("groups", None, "tensor", "seq"),
        check_vma=False,
    )
```

```python
import functools
import jax
import jax.numpy as jnp
from jax import lax
from jax.experimental import pallas as pl
from jax.experimental.pallas import tpu as pltpu
from jax.sharding import PartitionSpec as P

F32 = jnp.float32
BF16 = jnp.bfloat16
TILE = 256
CHUNKS = (256, 256, 256, 256, 256, 256, 256)


def silu_pair(gates):
    sigma = jax.nn.sigmoid(gates)
    return (gates * sigma, sigma * (1.0 + gates * (1.0 - sigma)))


def general(
    layer_input, out_grad, gate_pre, up_pre, w_down, proj_in, proj_ff, proj_down, lengths, slots
):
    tokens_here = layer_input.shape[0]
    tensor_count = lax.axis_size("tensor")
    share = 64 // tensor_count
    whole_down = lax.all_gather(w_down, "seq", axis=1, tiled=True)
    piece = lax.all_gather(out_grad, "tensor", axis=1, tiled=True)
    grad_total = lax.dot_general(
        piece, whole_down, (((1,), (1,)), ((), ())), preferred_element_type=F32
    )
    right_total = jnp.dot(piece, proj_down, preferred_element_type=F32)
    upper_value = up_pre.astype(F32)
    activated, slope = silu_pair(gate_pre.astype(F32))
    hidden = (activated * upper_value).astype(BF16)
    gate_grad = (grad_total * upper_value * slope).astype(BF16)
    up_grad = (grad_total * activated).astype(BF16)
    in_side = jnp.dot(layer_input, proj_in, preferred_element_type=F32)
    down_left = jnp.dot(hidden, proj_ff[:, 128:192], preferred_element_type=F32)
    gate_right = jnp.dot(gate_grad, proj_ff[:, 0:64], preferred_element_type=F32)
    up_right = jnp.dot(up_grad, proj_ff[:, 64:128], preferred_element_type=F32)
    left_local = jnp.concatenate([in_side, down_left], axis=1)
    right_local = jnp.concatenate([gate_right, up_right], axis=1)
    tensor_place = lax.axis_index("tensor")
    left_full, right_summed = lax.psum((left_local, right_local), "tensor")
    left_mine = lax.dynamic_slice_in_dim(
        left_full.reshape(tokens_here, 3, 64), tensor_place * share, share, 2
    )
    right_all = jnp.concatenate([right_summed, right_total], axis=1).reshape(tokens_here, 3, 64)
    examples = lengths.shape[0]
    positions = lax.axis_index("seq") * tokens_here + jnp.arange(tokens_here, dtype=jnp.int32)
    ends = jnp.cumsum(lengths)
    starts = ends - lengths
    member = (
        (positions[:, None] >= starts[None, :]) & (positions[:, None] < ends[None, :])
    ).astype(F32)
    scale = lax.rsqrt(lengths.astype(F32))
    sketches = []
    for linear in range(3):
        weighted = (member[:, :, None] * left_mine[:, None, linear, :]).reshape(
            tokens_here, examples * share
        )
        sketch = lax.dot_general(
            weighted,
            right_all[:, linear, :],
            (((0,), (0,)), ((), ())),
            precision=lax.Precision.HIGHEST,
            preferred_element_type=F32,
        )
        sketches.append(sketch.reshape(examples, share * 64))
    stacked = jnp.stack(sketches, axis=1) * scale[:, None, None]
    placing = (slots[None, :] == jnp.arange(examples, dtype=jnp.int32)[:, None]).astype(F32)
    placed = jnp.dot(
        placing,
        stacked.reshape(examples, 3 * share * 64),
        precision=lax.Precision.HIGHEST,
        preferred_element_type=F32,
    )
    return lax.psum_scatter(
        placed.reshape(examples, 3, share, 64), "seq", scatter_dimension=3, tiled=True
    )


def move_kernel(moves, n_in, *refs):
    scal, ins, refs = refs[0], refs[1 : 1 + n_in], refs[1 + n_in :]
    outs, (buf, sem) = refs[:-2], refs[-2:]
    y, at, steps = scal[2], 0, []
    for i, (src, lead, row, dst, to, rows) in enumerate(moves):
        a = ins[src] if lead is None else ins[src].at[y if lead == "y" else lead]
        a = a.at[pl.ds(row, rows)]
        mid = buf.at[pl.ds(at, rows)]
        steps.append(
            (
                pltpu.make_async_copy(a, mid, sem.at[0, i]),
                pltpu.make_async_copy(mid, outs[dst].at[pl.ds(to, rows)], sem.at[1, i]),
            )
        )
        at += rows
    for a, _ in steps:
        a.start()
    for a, b in steps:
        a.wait()
        b.start()
    for _, b in steps:
        b.wait()


def move(scal, ins, moves, out_rows):
    width, kind = ins[0].shape[-1], ins[0].dtype
    hbm = pl.BlockSpec(memory_space=pltpu.HBM)
    total = sum(m[-1] for m in moves)
    return pl.pallas_call(
        functools.partial(move_kernel, tuple(moves), len(ins)),
        out_shape=[jax.ShapeDtypeStruct((rows, width), kind) for rows in out_rows],
        in_specs=[pl.BlockSpec(memory_space=pltpu.SMEM)] + [hbm] * len(ins),
        out_specs=[hbm] * len(out_rows),
        scratch_shapes=[
            pltpu.VMEM((total, width), kind),
            pltpu.SemaphoreType.DMA((2, len(moves))),
        ],
        compiler_params=pltpu.CompilerParams(vmem_limit_bytes=60 * 1024 * 1024),
        cost_estimate=pl.CostEstimate(
            flops=0, bytes_accessed=4 * total * width, transcendentals=0
        ),
    )(scal, *ins)


def join(scal, pieces):
    moves, at = [], 0
    for i, piece in enumerate(pieces):
        moves.append((i, None, 0, 0, at, piece.shape[0]))
        at += piece.shape[0]
    return move(scal, pieces, moves, [at])[0]


def grads_kernel(tiles, half, first, last, *refs):
    n_pairs = 1 + max(t[0] for t in tiles)
    it = iter(refs)
    take = lambda n: [next(it) for _ in range(n)]
    (scal,) = take(1)
    (gathered,) = take(1)
    w_own, w_sib = take(2)
    pairs = [take(2) for _ in range(n_pairs)]
    gate, up, pg, pu = take(4)
    acc_in = None if first else take(2)
    if last:
        left_t, r_down, lo, hi, scale = take(5)
        keep, send = take(2)
    else:
        acc_out = take(2)
    og, wbuf, gbuf, ubuf, pbuf, grads, acc, og_sem, sems, p_sem = take(10)
    s, y = scal[0], scal[2]
    n = len(tiles)

    def fetch(t, slot, with_grad=False):
        for i, (pair, row, off, mine) in enumerate(tiles):
            if with_grad and i:
                break

            @pl.when(t == i)
            def _(pair=pair, row=row, off=off, mine=mine, i=i):
                h = (y, 1 - y, 0, 1)[mine]
                at = pl.multiple_of(h * half + off, 128)
                rows = pl.ds(at, TILE)
                here = pl.ds(row, TILE)
                a, b = pairs[pair]
                for j, src in enumerate(
                    (w_own.at[rows], w_sib.at[rows], a.at[here], b.at[here])
                ):
                    if with_grad:
                        pltpu.make_async_copy(gathered.at[s ^ j], og.at[s ^ j], og_sem.at[j]).start()
                    pltpu.make_async_copy(src, wbuf.at[slot, j], sems.at[slot, j]).start()
                pltpu.make_async_copy(gate.at[:, rows], gbuf.at[slot], sems.at[slot, 4]).start()
                pltpu.make_async_copy(up.at[:, rows], ubuf.at[slot], sems.at[slot, 5]).start()
                mine_p = pl.ds(i * TILE, TILE)
                pltpu.make_async_copy(pg.at[rows], pbuf.at[0, mine_p], p_sem).start()
                pltpu.make_async_copy(pu.at[rows], pbuf.at[1, mine_p], p_sem).start()

    def weights_arrive(slot, j):
        pltpu.make_async_copy(w_own.at[pl.ds(0, TILE)], wbuf.at[slot, j], sems.at[slot, j]).wait()

    def dots(slot, before):
        total = None
        for j in range(4):
            before(j)
            part = lax.dot_general(
                og[s ^ j],
                wbuf[slot, j],
                (((1,), (1,)), ((), ())),
                preferred_element_type=F32,
            )
            total = part if total is None else total + part
        return total

    def finish(t, slot, total):
        activated, slope = silu_pair(gbuf[slot].astype(F32))
        columns = pl.ds(pl.multiple_of(t * TILE, 128), TILE)
        grads[0, :, columns] = (total * ubuf[slot].astype(F32) * slope).astype(BF16)
        grads[1, :, columns] = (total * activated).astype(BF16)

    def streams_arrive(slot):
        rows = pl.ds(0, TILE)
        pltpu.make_async_copy(gate.at[:, rows], gbuf.at[slot], sems.at[slot, 4]).wait()
        pltpu.make_async_copy(up.at[:, rows], ubuf.at[slot], sems.at[slot, 5]).wait()

    fetch(jnp.int32(0), 0, True)
    fetch(jnp.int32(1), 1)
    for j in range(4):
        pltpu.make_async_copy(gathered.at[j], og.at[j], og_sem.at[j]).wait()

    @pl.loop(0, n)
    def _(t):
        slot = lax.rem(t, 3)
        @pl.when(t + 2 < n)
        def _():
            fetch(t + 2, lax.rem(t + 2, 3))
        for j in range(4):
            weights_arrive(slot, j)
        streams_arrive(slot)
        finish(t, slot, dots(slot, lambda j: None))

    every = pl.ds(0, n * TILE)
    pltpu.make_async_copy(pg.at[every], pbuf.at[0], p_sem).wait()
    pltpu.make_async_copy(pu.at[every], pbuf.at[1], p_sem).wait()

    @pl.loop(0, 2)
    def _(i):
        acc[i] = jnp.dot(grads[i], pbuf[i], preferred_element_type=F32)

    if not first:
        acc[0] += acc_in[0][...]
        acc[1] += acc_in[1][...]
    if not last:
        acc_out[0][...] = acc[0]
        acc_out[1][...] = acc[1]
        return
    acc[2] = r_down[...]
    tokens = acc.shape[1]
    where = s * tokens + lax.broadcasted_iota(jnp.int32, (tokens, 256), 0)
    weight = jnp.where((where >= lo[...]) & (where < hi[...]), scale[...], 0.0)
    even = lax.rem(s, 2) == 0

    @pl.loop(0, 3)
    def _(l):
        right = acc[l] * weight
        left = left_t[pl.ds(pl.multiple_of(64 * l, 64), 64), :]
        right_high, left_high = right.astype(BF16), left.astype(BF16)
        right_low = (right - right_high.astype(F32)).astype(BF16)
        left_low = (left - left_high.astype(F32)).astype(BF16)
        both = jnp.dot(
            jnp.concatenate([left_high, left_low]), right_high, preferred_element_type=F32
        )
        m = both[:64] + (
            both[64:] + jnp.dot(left_high, right_low, preferred_element_type=F32)
        )
        for x in range(2):
            a, b = m[:, 64 * x : 64 * x + 64], m[:, 128 + 64 * x : 192 + 64 * x]
            mine, other = jnp.where(even, a, b), jnp.where(even, b, a)
            for rows in range(4):
                part = slice(16 * rows, 16 * rows + 16)
                keep[x, rows, l] = mine[part]
                send[x, rows, l] = other[part]


def grads_call(tiles, half, scal, gathered, weights, pairs, streams, acc, tail):
    _, tokens, depth = gathered.shape
    first, last = acc is None, tail is not None
    hbm = pl.BlockSpec(memory_space=pltpu.HBM)
    vmem = pl.BlockSpec(memory_space=pltpu.VMEM)
    args = [scal, gathered, *weights, *[a for p in pairs for a in p], *streams]
    specs = [pl.BlockSpec(memory_space=pltpu.SMEM)] + [hbm] * (len(args) - 1)
    if not first:
        args += list(acc)
        specs += [vmem] * 2
    if last:
        args += list(tail)
        specs += [vmem] * len(tail)
        outs = [jax.ShapeDtypeStruct((2, 4, 3, 16, 64), F32)] * 2
    else:
        outs = [jax.ShapeDtypeStruct((tokens, 256), F32)] * 2
    units = len(tiles) * TILE
    return pl.pallas_call(
        functools.partial(grads_kernel, tiles, half, first, last),
        out_shape=outs,
        in_specs=specs,
        out_specs=[vmem] * 2,
        scratch_shapes=[
            pltpu.VMEM((4, tokens, depth), BF16),
            pltpu.VMEM((3, 4, TILE, depth), BF16),
            pltpu.VMEM((3, tokens, TILE), BF16),
            pltpu.VMEM((3, tokens, TILE), BF16),
            pltpu.VMEM((2, units, 256), BF16),
            pltpu.VMEM((2, tokens, units), BF16),
            pltpu.VMEM((3, tokens, 256), F32),
            pltpu.SemaphoreType.DMA((4,)),
            pltpu.SemaphoreType.DMA((3, 6)),
            pltpu.SemaphoreType.DMA,
        ],
        compiler_params=pltpu.CompilerParams(vmem_limit_bytes=60 * 1024 * 1024),
        cost_estimate=pl.CostEstimate(
            flops=2 * units * tokens * (4 * depth + 512),
            bytes_accessed=2 * (4 * tokens * depth + units * (4 * depth + 2 * tokens)),
            transcendentals=units * tokens,
        ),
    )(*args)


def local(
    layer_input, out_grad, gate_pre, up_pre, w_down, proj_in, proj_ff, proj_down, lengths, slots
):
    tokens = layer_input.shape[0]
    depth = out_grad.shape[1]
    units = w_down.shape[0]
    half = units // 2
    y, s, z = (lax.axis_index(a) for a in ("groups", "seq", "tensor"))
    scal = jnp.stack([s, z, y]).astype(jnp.int32)

    over_x = lambda a: lax.ppermute(a, "seq", [(i, i ^ 2) for i in range(4)])
    over_c = lambda a: lax.ppermute(a, "seq", [(i, i ^ 1) for i in range(4)])
    over_y = lambda a: lax.ppermute(a, "groups", [(0, 1), (1, 0)])
    over_z = lambda a, k: lax.ppermute(a, "tensor", [(i, i ^ k) for i in range(4)])

    count = len(CHUNKS)
    offs = [sum(CHUNKS[:k]) for k in range(count)]
    r, ry = [None] * (count + 1), [None] * count
    tie = lax.optimization_barrier
    halves = w_down.reshape(2, half, depth)
    whole = count - 1
    sources = [("y", k) for k in range(whole)] + [(0, whole), (1, whole)]
    cut = lambda picks: move(
        scal,
        [halves],
        [(0, h, offs[k], i, 0, CHUNKS[k]) for i, (h, k) in enumerate(picks)],
        [CHUNKS[k] for _, k in picks],
    )

    gathered = lax.all_gather(out_grad, "tensor", axis=0, tiled=False)
    r[0] = over_x(cut(sources[:1])[0])
    srcs = [None] + list(cut(sources[1:]))
    now = srcs[2:]
    r[1] = over_x(srcs[1])
    w_sib = over_c(w_down)

    column = jnp.arange(64, dtype=jnp.int32)[:, None]
    lane = jnp.arange(256, dtype=jnp.int32)[None, :]
    source = (2 * ((lane // 64) % 2) + lane // 128) * 16 + lane % 16
    spread = (column == source).astype(BF16)
    expand = lambda a: jnp.dot(a, spread, preferred_element_type=F32).astype(BF16)
    ends = jnp.cumsum(lengths)
    pick = slots[:, None] == (lane // 16) % 4
    by_lane = lambda a: jnp.sum(jnp.where(pick, a[:, None], jnp.zeros((), a.dtype)), 0, keepdims=True)
    lo, hi = by_lane(ends - lengths), by_lane(ends)
    scale = by_lane(lax.rsqrt(lengths.astype(F32)))

    swap_after = {
        0: ((0, 0),),
        2: ((0, 1),),
        4: ((1, 0),),
        5: ((1, 1), (2, 0), (2, 1), (3, 0), (3, 1), (4, 0), (5, 0)),
        6: ((4, 1), (5, 1), (6, 0)),
    }
    swapped_by = {2: 0, 4: 1, 6: 2}
    pairs, where = [], {}

    def swap(members, across=True):
        rows = 0
        for k, far in members:
            for row in range(0, CHUNKS[min(k, whole)], TILE):
                where[(k, far, row)] = (len(pairs), rows)
                rows += TILE
        got = [ry[k] if far else r[k] for k, far in members]
        got = got[0] if len(got) == 1 else join(scal, got)
        pairs.append((got, over_c(got)) if across else got)

    for k in range(count):
        final = k == count - 1
        gate = {"now": now, "r": r[k]}
        if k == 0:
            gate["left"] = (layer_input, gate_pre, up_pre)
        if k == 2:
            gate["left"], gate["lanes"] = left_t, (lo, hi, scale)
        if k == count - 2:
            gate["side"] = (proj_ff, proj_down, left_t)
        if k in swapped_by:
            gate["c"] = pairs[swapped_by[k]]
        if final:
            gate["side"], gate["left"] = side, left_t
        if k == 1:
            gate["sib"] = w_sib
        if k >= 2:
            gate["y"] = ry[k - 2]
        if final:
            gate["y5"], gate["all"] = ry[k - 1], gathered
            gate["join"] = pairs[3]
        gate = tie(gate)
        now, r[k] = gate["now"], gate["r"]
        if k + 2 <= count:
            r[k + 2] = over_x(now[0])
            now = now[1:]
        if k >= 2:
            ry[k - 2] = gate["y"]
        if k == 1:
            w_sib = gate["sib"]
        if not final:
            ry[k] = over_y(r[k])
        if k == 0:
            tokens_in, gates, uppers = gate["left"]
            activated, _ = silu_pair(gates.astype(F32))
            hidden = (activated * uppers.astype(F32)).astype(BF16)
            in_side = jnp.dot(tokens_in, proj_in, preferred_element_type=F32)
            down_left = jnp.dot(hidden, proj_ff[:, 128:192], preferred_element_type=F32)
            left_t = jnp.concatenate([in_side, down_left], axis=1).T
        if k == 2:
            left_t, (lo, hi, scale) = gate["left"], gate["lanes"]
        if k == count - 2:
            ff, down, left_t = gate["side"]
            left_t = (left_t, over_z(left_t.astype(BF16), 1))
            down_rows = lax.dynamic_slice_in_dim(down, z * depth, depth, 0)
            side = (
                expand(ff[:, 0:64]),
                expand(ff[:, 64:128]),
                jnp.dot(out_grad, expand(down_rows), preferred_element_type=F32),
            )
        if final:
            pg, pu, r_down = gate["side"]
            left_t = gate["left"][0] + gate["left"][1].astype(F32)
            left_t = left_t + over_z(left_t.astype(BF16), 2).astype(F32)
            ry[k - 1], gathered = gate["y5"], gate["all"]
        if k in swapped_by:
            pairs[swapped_by[k]] = gate["c"]
        if final:
            pairs[3] = (gate["join"], over_c(gate["join"]))
        if k in swap_after:
            swap(swap_after[k], k != 5)

    def grads(members, acc, tail=None):
        used, tiles = [], []
        for k, far in members:
            at_half = min(k, whole)
            for row in range(0, CHUNKS[at_half], TILE):
                pair, at = where[(k, far, row)]
                if pair not in used:
                    used.append(pair)
                half_of = far if k < whole else 2 + k - whole
                tiles.append((used.index(pair), at, offs[at_half] + row, half_of))
        return grads_call(
            tuple(tiles), half, scal, gathered, (w_down, w_sib), [pairs[p] for p in used],
            (gate_pre, up_pre, pg, pu), acc, tail,
        )

    early, late = ((0, 0), (0, 1), (1, 0)), swap_after[5] + swap_after[6]
    acc = grads(early, None)
    r[7], left_t, acc = tie((r[7], left_t, acc))
    swap(((7, 0),))
    acc = grads(late + ((7, 0),), acc, (left_t, r_down, lo, hi, scale))
    keep, send = acc
    x = s // 2
    part = lambda a, at: lax.dynamic_index_in_dim(a, at, 0, keepdims=False)
    total = keep + over_c(send)
    total = part(total, x) + over_x(part(total, 1 - x))
    total = total.reshape(2, 2, 3, 16, 64)
    total = part(total, z // 2) + over_z(part(total, 1 - z // 2), 2)
    total = part(total, z % 2) + over_z(part(total, 1 - z % 2), 1)
    return total.reshape(3, 16, 4, 16).transpose(2, 0, 1, 3)


def solution(mesh):
    placed = (
        P(("groups", "seq"), "tensor"),
        P(("groups", "seq"), "tensor"),
        P(("groups", "seq"), "tensor"),
        P(("groups", "seq"), "tensor"),
        P("tensor", "seq"),
        P("tensor", None),
        P("tensor", None),
        P(),
        P("groups"),
        P("groups"),
    )
    small = (mesh.shape["groups"], mesh.shape["seq"], mesh.shape["tensor"]) == (2, 4, 4)
    return jax.shard_map(
        local if small else general,
        mesh=mesh,
        in_specs=placed,
        out_specs=P("groups", None, "tensor", "seq"),
        check_vma=False,
    )
```

```python
import functools
import jax
import jax.numpy as jnp
from jax import lax
from jax.experimental import pallas as pl
from jax.experimental.pallas import tpu as pltpu
from jax.sharding import PartitionSpec as P

F32 = jnp.float32
BF16 = jnp.bfloat16
TILE = 256
CHUNKS = (256, 256, 256, 256, 256, 256, 256)


def silu_pair(gates):
    sigma = jax.nn.sigmoid(gates)
    return (gates * sigma, sigma * (1.0 + gates * (1.0 - sigma)))


def general(
    layer_input, out_grad, gate_pre, up_pre, w_down, proj_in, proj_ff, proj_down, lengths, slots
):
    tokens_here = layer_input.shape[0]
    tensor_count = lax.axis_size("tensor")
    share = 64 // tensor_count
    whole_down = lax.all_gather(w_down, "seq", axis=1, tiled=True)
    piece = lax.all_gather(out_grad, "tensor", axis=1, tiled=True)
    grad_total = lax.dot_general(
        piece, whole_down, (((1,), (1,)), ((), ())), preferred_element_type=F32
    )
    right_total = jnp.dot(piece, proj_down, preferred_element_type=F32)
    upper_value = up_pre.astype(F32)
    activated, slope = silu_pair(gate_pre.astype(F32))
    hidden = (activated * upper_value).astype(BF16)
    gate_grad = (grad_total * upper_value * slope).astype(BF16)
    up_grad = (grad_total * activated).astype(BF16)
    in_side = jnp.dot(layer_input, proj_in, preferred_element_type=F32)
    down_left = jnp.dot(hidden, proj_ff[:, 128:192], preferred_element_type=F32)
    gate_right = jnp.dot(gate_grad, proj_ff[:, 0:64], preferred_element_type=F32)
    up_right = jnp.dot(up_grad, proj_ff[:, 64:128], preferred_element_type=F32)
    left_local = jnp.concatenate([in_side, down_left], axis=1)
    right_local = jnp.concatenate([gate_right, up_right], axis=1)
    tensor_place = lax.axis_index("tensor")
    left_full, right_summed = lax.psum((left_local, right_local), "tensor")
    left_mine = lax.dynamic_slice_in_dim(
        left_full.reshape(tokens_here, 3, 64), tensor_place * share, share, 2
    )
    right_all = jnp.concatenate([right_summed, right_total], axis=1).reshape(tokens_here, 3, 64)
    examples = lengths.shape[0]
    positions = lax.axis_index("seq") * tokens_here + jnp.arange(tokens_here, dtype=jnp.int32)
    ends = jnp.cumsum(lengths)
    starts = ends - lengths
    member = (
        (positions[:, None] >= starts[None, :]) & (positions[:, None] < ends[None, :])
    ).astype(F32)
    scale = lax.rsqrt(lengths.astype(F32))
    sketches = []
    for linear in range(3):
        weighted = (member[:, :, None] * left_mine[:, None, linear, :]).reshape(
            tokens_here, examples * share
        )
        sketch = lax.dot_general(
            weighted,
            right_all[:, linear, :],
            (((0,), (0,)), ((), ())),
            precision=lax.Precision.HIGHEST,
            preferred_element_type=F32,
        )
        sketches.append(sketch.reshape(examples, share * 64))
    stacked = jnp.stack(sketches, axis=1) * scale[:, None, None]
    placing = (slots[None, :] == jnp.arange(examples, dtype=jnp.int32)[:, None]).astype(F32)
    placed = jnp.dot(
        placing,
        stacked.reshape(examples, 3 * share * 64),
        precision=lax.Precision.HIGHEST,
        preferred_element_type=F32,
    )
    return lax.psum_scatter(
        placed.reshape(examples, 3, share, 64), "seq", scatter_dimension=3, tiled=True
    )


def move_kernel(moves, n_in, *refs):
    ins, refs = refs[:n_in], refs[n_in:]
    outs, (buf, sem) = refs[:-2], refs[-2:]
    y, at, steps = lax.axis_index("groups"), 0, []
    for i, (src, lead, row, dst, to, rows) in enumerate(moves):
        a = ins[src] if lead is None else ins[src].at[y if lead == "y" else lead]
        a = a.at[pl.ds(row, rows)]
        mid = buf.at[pl.ds(at, rows)]
        steps.append(
            (
                pltpu.make_async_copy(a, mid, sem.at[0, i]),
                pltpu.make_async_copy(mid, outs[dst].at[pl.ds(to, rows)], sem.at[1, i]),
            )
        )
        at += rows
    for a, _ in steps:
        a.start()
    for a, b in steps:
        a.wait()
        b.start()
    for _, b in steps:
        b.wait()


def move(scal, ins, moves, out_rows):
    width, kind = ins[0].shape[-1], ins[0].dtype
    hbm = pl.BlockSpec(memory_space=pltpu.HBM)
    total = sum(m[-1] for m in moves)
    return pl.pallas_call(
        functools.partial(move_kernel, tuple(moves), len(ins)),
        out_shape=[jax.ShapeDtypeStruct((rows, width), kind) for rows in out_rows],
        in_specs=[hbm] * len(ins),
        out_specs=[hbm] * len(out_rows),
        scratch_shapes=[
            pltpu.VMEM((total, width), kind),
            pltpu.SemaphoreType.DMA((2, len(moves))),
        ],
        compiler_params=pltpu.CompilerParams(vmem_limit_bytes=60 * 1024 * 1024),
        cost_estimate=pl.CostEstimate(
            flops=0, bytes_accessed=4 * total * width, transcendentals=0
        ),
    )(*ins)


def join(scal, pieces):
    moves, at = [], 0
    for i, piece in enumerate(pieces):
        moves.append((i, None, 0, 0, at, piece.shape[0]))
        at += piece.shape[0]
    return move(scal, pieces, moves, [at])[0]


def grads_kernel(tiles, half, first, last, *refs):
    n_pairs = 1 + max(t[0] for t in tiles)
    it = iter(refs)
    take = lambda n: [next(it) for _ in range(n)]
    (scal,) = take(1)
    (gathered,) = take(1)
    w_own, w_sib = take(2)
    pairs = [take(2) for _ in range(n_pairs)]
    gate, up, pg, pu = take(4)
    acc_in = None if first else take(2)
    if last:
        left_t, r_down, lo, hi, scale = take(5)
        keep, send = take(2)
    else:
        acc_out = take(2)
    og, wbuf, gbuf, ubuf, pbuf, grads, acc, og_sem, sems, p_sem = take(10)
    s, y = scal[0], scal[2]
    n = len(tiles)

    def fetch(t, slot, with_grad=False):
        for i, (pair, row, off, mine) in enumerate(tiles):
            if with_grad and i:
                break

            @pl.when(t == i)
            def _(pair=pair, row=row, off=off, mine=mine, i=i):
                h = (y, 1 - y, 0, 1)[mine]
                at = pl.multiple_of(h * half + off, 128)
                rows = pl.ds(at, TILE)
                here = pl.ds(row, TILE)
                a, b = pairs[pair]
                for j, src in enumerate(
                    (w_own.at[rows], w_sib.at[rows], a.at[here], b.at[here])
                ):
                    if with_grad:
                        pltpu.make_async_copy(gathered.at[s ^ j], og.at[s ^ j], og_sem.at[j]).start()
                    pltpu.make_async_copy(src, wbuf.at[slot, j], sems.at[slot, j]).start()
                pltpu.make_async_copy(gate.at[:, rows], gbuf.at[slot], sems.at[slot, 4]).start()
                pltpu.make_async_copy(up.at[:, rows], ubuf.at[slot], sems.at[slot, 5]).start()
                mine_p = pl.ds(i * TILE, TILE)
                pltpu.make_async_copy(pg.at[rows], pbuf.at[0, mine_p], p_sem).start()
                pltpu.make_async_copy(pu.at[rows], pbuf.at[1, mine_p], p_sem).start()

    def weights_arrive(slot, j):
        pltpu.make_async_copy(w_own.at[pl.ds(0, TILE)], wbuf.at[slot, j], sems.at[slot, j]).wait()

    def dots(slot, before):
        total = None
        for j in range(4):
            before(j)
            part = lax.dot_general(
                og[s ^ j],
                wbuf[slot, j],
                (((1,), (1,)), ((), ())),
                preferred_element_type=F32,
            )
            total = part if total is None else total + part
        return total

    def finish(t, slot, total):
        activated, slope = silu_pair(gbuf[slot].astype(F32))
        columns = pl.ds(pl.multiple_of(t * TILE, 128), TILE)
        grads[0, :, columns] = (total * ubuf[slot].astype(F32) * slope).astype(BF16)
        grads[1, :, columns] = (total * activated).astype(BF16)

    def streams_arrive(slot):
        rows = pl.ds(0, TILE)
        pltpu.make_async_copy(gate.at[:, rows], gbuf.at[slot], sems.at[slot, 4]).wait()
        pltpu.make_async_copy(up.at[:, rows], ubuf.at[slot], sems.at[slot, 5]).wait()

    fetch(jnp.int32(0), 0, True)
    fetch(jnp.int32(1), 1)
    for j in range(4):
        pltpu.make_async_copy(gathered.at[j], og.at[j], og_sem.at[j]).wait()

    @pl.loop(0, n)
    def _(t):
        slot = lax.rem(t, 3)
        @pl.when(t + 2 < n)
        def _():
            fetch(t + 2, lax.rem(t + 2, 3))
        for j in range(4):
            weights_arrive(slot, j)
        streams_arrive(slot)
        finish(t, slot, dots(slot, lambda j: None))

    every = pl.ds(0, n * TILE)
    pltpu.make_async_copy(pg.at[every], pbuf.at[0], p_sem).wait()
    pltpu.make_async_copy(pu.at[every], pbuf.at[1], p_sem).wait()

    @pl.loop(0, 2)
    def _(i):
        acc[i] = jnp.dot(grads[i], pbuf[i], preferred_element_type=F32)

    if not first:
        acc[0] += acc_in[0][...]
        acc[1] += acc_in[1][...]
    if not last:
        acc_out[0][...] = acc[0]
        acc_out[1][...] = acc[1]
        return
    acc[2] = r_down[...]
    tokens = acc.shape[1]
    where = s * tokens + lax.broadcasted_iota(jnp.int32, (tokens, 256), 0)
    weight = jnp.where((where >= lo[...]) & (where < hi[...]), scale[...], 0.0)
    even = lax.rem(s, 2) == 0

    @pl.loop(0, 3)
    def _(l):
        right = acc[l] * weight
        left = left_t[pl.ds(pl.multiple_of(64 * l, 64), 64), :]
        right_high, left_high = right.astype(BF16), left.astype(BF16)
        right_low = (right - right_high.astype(F32)).astype(BF16)
        left_low = (left - left_high.astype(F32)).astype(BF16)
        both = jnp.dot(
            jnp.concatenate([left_high, left_low]), right_high, preferred_element_type=F32
        )
        m = both[:64] + (
            both[64:] + jnp.dot(left_high, right_low, preferred_element_type=F32)
        )
        for x in range(2):
            a, b = m[:, 64 * x : 64 * x + 64], m[:, 128 + 64 * x : 192 + 64 * x]
            mine, other = jnp.where(even, a, b), jnp.where(even, b, a)
            for rows in range(4):
                part = slice(16 * rows, 16 * rows + 16)
                keep[x, rows, l] = mine[part]
                send[x, rows, l] = other[part]


def grads_call(tiles, half, scal, gathered, weights, pairs, streams, acc, tail):
    _, tokens, depth = gathered.shape
    first, last = acc is None, tail is not None
    hbm = pl.BlockSpec(memory_space=pltpu.HBM)
    vmem = pl.BlockSpec(memory_space=pltpu.VMEM)
    args = [scal, gathered, *weights, *[a for p in pairs for a in p], *streams]
    specs = [pl.BlockSpec(memory_space=pltpu.SMEM)] + [hbm] * (len(args) - 1)
    if not first:
        args += list(acc)
        specs += [vmem] * 2
    if last:
        args += list(tail)
        specs += [vmem] * len(tail)
        outs = [jax.ShapeDtypeStruct((2, 4, 3, 16, 64), F32)] * 2
    else:
        outs = [jax.ShapeDtypeStruct((tokens, 256), F32)] * 2
    units = len(tiles) * TILE
    return pl.pallas_call(
        functools.partial(grads_kernel, tiles, half, first, last),
        out_shape=outs,
        in_specs=specs,
        out_specs=[vmem] * 2,
        scratch_shapes=[
            pltpu.VMEM((4, tokens, depth), BF16),
            pltpu.VMEM((3, 4, TILE, depth), BF16),
            pltpu.VMEM((3, tokens, TILE), BF16),
            pltpu.VMEM((3, tokens, TILE), BF16),
            pltpu.VMEM((2, units, 256), BF16),
            pltpu.VMEM((2, tokens, units), BF16),
            pltpu.VMEM((3, tokens, 256), F32),
            pltpu.SemaphoreType.DMA((4,)),
            pltpu.SemaphoreType.DMA((3, 6)),
            pltpu.SemaphoreType.DMA,
        ],
        compiler_params=pltpu.CompilerParams(vmem_limit_bytes=60 * 1024 * 1024),
        cost_estimate=pl.CostEstimate(
            flops=2 * units * tokens * (4 * depth + 512),
            bytes_accessed=2 * (4 * tokens * depth + units * (4 * depth + 2 * tokens)),
            transcendentals=units * tokens,
        ),
    )(*args)


def local(
    layer_input, out_grad, gate_pre, up_pre, w_down, proj_in, proj_ff, proj_down, lengths, slots
):
    tokens = layer_input.shape[0]
    depth = out_grad.shape[1]
    units = w_down.shape[0]
    half = units // 2
    y, s, z = (lax.axis_index(a) for a in ("groups", "seq", "tensor"))
    scal = jnp.stack([s, z, y]).astype(jnp.int32)

    over_x = lambda a: lax.ppermute(a, "seq", [(i, i ^ 2) for i in range(4)])
    over_c = lambda a: lax.ppermute(a, "seq", [(i, i ^ 1) for i in range(4)])
    over_y = lambda a: lax.ppermute(a, "groups", [(0, 1), (1, 0)])
    over_z = lambda a, k: lax.ppermute(a, "tensor", [(i, i ^ k) for i in range(4)])

    count = len(CHUNKS)
    offs = [sum(CHUNKS[:k]) for k in range(count)]
    r, ry = [None] * (count + 1), [None] * count
    tie = lax.optimization_barrier
    halves = w_down.reshape(2, half, depth)
    whole = count - 1
    sources = [("y", k) for k in range(whole)] + [(0, whole), (1, whole)]
    cut = lambda picks: move(
        scal,
        [halves],
        [(0, h, offs[k], i, 0, CHUNKS[k]) for i, (h, k) in enumerate(picks)],
        [CHUNKS[k] for _, k in picks],
    )

    gathered = lax.all_gather(out_grad, "tensor", axis=0, tiled=False)
    r[0] = over_x(cut(sources[:1])[0])
    srcs = [None] + list(cut(sources[1:]))
    now = srcs[2:]
    r[1] = over_x(srcs[1])
    w_sib = over_c(w_down)

    column = jnp.arange(64, dtype=jnp.int32)[:, None]
    lane = jnp.arange(256, dtype=jnp.int32)[None, :]
    source = (2 * ((lane // 64) % 2) + lane // 128) * 16 + lane % 16
    spread = (column == source).astype(BF16)
    expand = lambda a: jnp.dot(a, spread, preferred_element_type=F32).astype(BF16)
    ends = jnp.cumsum(lengths)
    pick = slots[:, None] == (lane // 16) % 4
    by_lane = lambda a: jnp.sum(jnp.where(pick, a[:, None], jnp.zeros((), a.dtype)), 0, keepdims=True)
    lo, hi = by_lane(ends - lengths), by_lane(ends)
    scale = by_lane(lax.rsqrt(lengths.astype(F32)))

    swap_after = {
        0: ((0, 0),),
        2: ((0, 1),),
        4: ((1, 0),),
        5: ((1, 1), (2, 0), (2, 1), (3, 0), (3, 1), (4, 0), (5, 0)),
        6: ((4, 1), (5, 1), (6, 0)),
    }
    swapped_by = {2: 0, 4: 1, 6: 2}
    pairs, where = [], {}

    def swap(members, across=True):
        rows = 0
        for k, far in members:
            for row in range(0, CHUNKS[min(k, whole)], TILE):
                where[(k, far, row)] = (len(pairs), rows)
                rows += TILE
        got = [ry[k] if far else r[k] for k, far in members]
        got = got[0] if len(got) == 1 else join(scal, got)
        pairs.append((got, over_c(got)) if across else got)

    for k in range(count):
        final = k == count - 1
        gate = {"now": now, "r": r[k]}
        if k == 0:
            gate["left"] = (layer_input, gate_pre, up_pre)
        if k == 2:
            gate["left"], gate["lanes"] = left_t, (lo, hi, scale)
        if k == count - 2:
            gate["side"] = (proj_ff, proj_down, left_t)
        if k in swapped_by:
            gate["c"] = pairs[swapped_by[k]]
        if final:
            gate["side"], gate["left"] = side, left_t
        if k == 1:
            gate["sib"] = w_sib
        if k >= 2:
            gate["y"] = ry[k - 2]
        if final:
            gate["y5"], gate["all"] = ry[k - 1], gathered
            gate["join"] = pairs[3]
        gate = tie(gate)
        now, r[k] = gate["now"], gate["r"]
        if k + 2 <= count:
            r[k + 2] = over_x(now[0])
            now = now[1:]
        if k >= 2:
            ry[k - 2] = gate["y"]
        if k == 1:
            w_sib = gate["sib"]
        if not final:
            ry[k] = over_y(r[k])
        if k == 0:
            tokens_in, gates, uppers = gate["left"]
            activated, _ = silu_pair(gates.astype(F32))
            hidden = (activated * uppers.astype(F32)).astype(BF16)
            in_side = jnp.dot(tokens_in, proj_in, preferred_element_type=F32)
            down_left = jnp.dot(hidden, proj_ff[:, 128:192], preferred_element_type=F32)
            left_t = jnp.concatenate([in_side, down_left], axis=1).T
        if k == 2:
            left_t, (lo, hi, scale) = gate["left"], gate["lanes"]
        if k == count - 2:
            ff, down, left_t = gate["side"]
            left_t = (left_t, over_z(left_t.astype(BF16), 1))
            down_rows = lax.dynamic_slice_in_dim(down, z * depth, depth, 0)
            side = (
                expand(ff[:, 0:64]),
                expand(ff[:, 64:128]),
                jnp.dot(out_grad, expand(down_rows), preferred_element_type=F32),
            )
        if final:
            pg, pu, r_down = gate["side"]
            left_t = gate["left"][0] + gate["left"][1].astype(F32)
            left_t = left_t + over_z(left_t.astype(BF16), 2).astype(F32)
            ry[k - 1], gathered = gate["y5"], gate["all"]
        if k in swapped_by:
            pairs[swapped_by[k]] = gate["c"]
        if final:
            pairs[3] = (gate["join"], over_c(gate["join"]))
        if k in swap_after:
            swap(swap_after[k], k != 5)

    def grads(members, acc, tail=None):
        used, tiles = [], []
        for k, far in members:
            at_half = min(k, whole)
            for row in range(0, CHUNKS[at_half], TILE):
                pair, at = where[(k, far, row)]
                if pair not in used:
                    used.append(pair)
                half_of = far if k < whole else 2 + k - whole
                tiles.append((used.index(pair), at, offs[at_half] + row, half_of))
        return grads_call(
            tuple(tiles), half, scal, gathered, (w_down, w_sib), [pairs[p] for p in used],
            (gate_pre, up_pre, pg, pu), acc, tail,
        )

    early, late = ((0, 0), (0, 1), (1, 0)), swap_after[5] + swap_after[6]
    acc = grads(early, None)
    r[7], left_t, acc = tie((r[7], left_t, acc))
    swap(((7, 0),))
    acc = grads(late + ((7, 0),), acc, (left_t, r_down, lo, hi, scale))
    keep, send = acc
    x = s // 2
    part = lambda a, at: lax.dynamic_index_in_dim(a, at, 0, keepdims=False)
    total = keep + over_c(send)
    total = part(total, x) + over_x(part(total, 1 - x))
    total = total.reshape(2, 2, 3, 16, 64)
    total = part(total, z // 2) + over_z(part(total, 1 - z // 2), 2)
    total = part(total, z % 2) + over_z(part(total, 1 - z % 2), 1)
    return total.reshape(3, 16, 4, 16).transpose(2, 0, 1, 3)


def solution(mesh):
    placed = (
        P(("groups", "seq"), "tensor"),
        P(("groups", "seq"), "tensor"),
        P(("groups", "seq"), "tensor"),
        P(("groups", "seq"), "tensor"),
        P("tensor", "seq"),
        P("tensor", None),
        P("tensor", None),
        P(),
        P("groups"),
        P("groups"),
    )
    small = (mesh.shape["groups"], mesh.shape["seq"], mesh.shape["tensor"]) == (2, 4, 4)
    return jax.shard_map(
        local if small else general,
        mesh=mesh,
        in_specs=placed,
        out_specs=P("groups", None, "tensor", "seq"),
        check_vma=False,
    )
```
